32 devices in a mesh: seq: 8 (over z, core), table: 4 (over y, x).
Axes of the slice: x: 2, y: 2, z: 4, core: 2. Of those that a mesh axis runs over, the one named last changes fastest.
Arguments:
- columns: bfloat16 [4, 2048, 512], P(None, 'seq', 'table'), may hold values from -6 to 6
- gaps: float32 [4, 2048], P('table', 'seq'), may hold values from 0.2 to 2457.6
- norm_in: float32 [512], replicated, may hold values from 0.1 to 1.9
- w_gate: bfloat16 [512, 1024], replicated, may hold values from -0.25 to 0.25
- w_xbc: bfloat16 [512, 1280], replicated, may hold values from -0.25 to 0.25
- w_step: bfloat16 [512, 16], replicated, may hold values from -0.25 to 0.25
- step_bias: float32 [16], replicated, may hold values from -1 to 1
- conv_weight: float32 [4, 1280], replicated, may hold values from -1 to 1
- conv_bias: float32 [1280], replicated, may hold values from -1.5 to 1.5
- rates: float32 [16], replicated, may hold values from 2.4414063e-05 to 0.04
- norm_out: float32 [1024], replicated, may hold values from 0.1 to 1.9
- w_out: bfloat16 [1024, 512], replicated, may hold values from -0.1875 to 0.1875
Outputs:
- mixed: bfloat16 [4, 2048, 512], P('table', 'seq')
The draws below stay inside these ranges and needn't reach their ends.
All inputs are finite; a program needn't handle non-finite values.
Results may differ from the reference program's by a relative error of at most 0.02.
Values may be sent and summed in bfloat16 or wider, within the bound.
A program may use at most 64 MiB of HBM per device.

```python
import math
import jax
import jax.numpy as jnp
from jax import lax

D = 512
HEADS = 16
HEAD_DIM = 64
STATE = 128
BLOCK = 256
CONV = 4
INNER = 1024
SEQ_DEV = 256
HISTS = 4
LEN = 2048


def draw_gaps(key, part):
    first = jax.random.fold_in(key, 11)
    second = jax.random.fold_in(key, 12)
    third = jax.random.fold_in(key, 13)
    span = SEQ_DEV // 2
    count = LEN // span
    levels = jnp.exp(jax.random.uniform(first, (HISTS, count), jnp.float32, math.log(0.4), math.log(3.2)))
    jitter = jnp.exp(jax.random.uniform(second, (HISTS, LEN), jnp.float32, math.log(0.5), math.log(2.0)))
    spread = jnp.repeat(levels, span, axis=1) * jitter
    places = jax.random.randint(third, (HISTS, 3, 1), 0, LEN)
    marks = jnp.any(places == jnp.arange(LEN)[None, None, :], axis=1)
    return jnp.where(marks, 1.2 * LEN, spread).astype(jnp.float32)


def draw_rates(key, part):
    first = jax.random.fold_in(key, 21)
    second = jax.random.fold_in(key, 22)
    third = jax.random.fold_in(key, 23)
    order = jax.random.permutation(first, HEADS)
    edge = math.log(2.0 / LEN)
    top = math.log(0.039)
    half = HEADS // 2
    quick_heads = order < half
    place = (order.astype(jnp.float32) + jax.random.uniform(second, (HEADS,), jnp.float32, 0.0, 1.0)) / half
    quick = jnp.exp(edge + jnp.minimum(place, 1.0) * (top - edge))
    slow = jnp.exp(jax.random.uniform(third, (HEADS,), jnp.float32, math.log(0.06 / LEN), edge))
    return jnp.where(quick_heads, quick, slow).astype(jnp.float32)


def draw_conv_weight(key, part):
    raw = jax.random.normal(jax.random.fold_in(key, 31), (CONV, INNER + 2 * STATE), jnp.float32)
    length = jnp.sqrt(jnp.sum(raw * raw, axis=0, keepdims=True))
    return (raw / jnp.maximum(length, 0.5)).astype(jnp.float32)


def draw_conv_bias(key, part):
    width = INNER + 2 * STATE
    centred = jax.random.uniform(jax.random.fold_in(key, 41), (width,), jnp.float32, -0.15, 0.15) - 0.55
    spread = jax.random.uniform(jax.random.fold_in(key, 42), (width,), jnp.float32, -1.5, 1.5)
    channel = jnp.arange(width)
    return jnp.where(channel < INNER + STATE, centred, spread).astype(jnp.float32)


def shard_levels(own_key, extent, shards, least, high):
    factor_of = 1.0
    for position, parts in shards:
        steps = jax.random.uniform(jax.random.fold_in(jax.random.fold_in(own_key, 6), position), (parts,), jnp.float32, least / len(shards), high / len(shards))
        factor_of = factor_of * jnp.repeat(jnp.exp(steps), extent[position] // parts).reshape((-1,) + (1,) * (len(extent) - 1 - position))
    return factor_of


def normal_values(stream_key, shape, deviation, most, cuts=(), dtype=jnp.bfloat16):
    array = deviation * jax.random.normal(stream_key, shape, jnp.float32)
    if cuts:
        array = array * shard_levels(stream_key, shape, cuts, -0.22, 0.18)
    return jnp.clip(array, -most, most).astype(dtype)


def setup_inputs(seed: int = 0) -> dict:
    streams_of = jax.random.split(jax.random.key(seed), 13)
    return {
        "columns": normal_values(streams_of[0], (HISTS, LEN, D), 1.0, 6.0, ((1, 8), (2, 4))),
        "gaps": draw_gaps(jax.random.fold_in(streams_of[12], 71), 0),
        "norm_in": jnp.clip(1.0 + 0.18 * jax.random.normal(streams_of[2], (D,), jnp.float32), 0.1, 1.9),
        "w_gate": normal_values(streams_of[3], (D, INNER), D ** -0.5, 0.25),
        "w_xbc": normal_values(streams_of[4], (D, INNER + 2 * STATE), D ** -0.5, 0.25),
        "w_step": normal_values(streams_of[5], (D, HEADS), D ** -0.5, 0.25),
        "step_bias": jnp.clip(jax.random.uniform(streams_of[6], (HEADS,), jnp.float32, -1.0, 1.0), -1.0, 1.0),
        "conv_weight": draw_conv_weight(jax.random.fold_in(streams_of[12], 71), 0),
        "conv_bias": draw_conv_bias(jax.random.fold_in(streams_of[12], 71), 0),
        "rates": draw_rates(jax.random.fold_in(streams_of[12], 71), 0),
        "norm_out": jnp.clip(1.0 + 0.18 * jax.random.normal(streams_of[10], (INNER,), jnp.float32), 0.1, 1.9),
        "w_out": normal_values(streams_of[11], (INNER, D), INNER ** -0.5, 0.1875),
    }


epsilon = 1e-05

def rms_rows(values, gain):
    return values * lax.rsqrt(lax.optimization_barrier(jnp.mean(values * values, axis=-1, keepdims=True)) + epsilon) * gain

def history(columns_one, gaps_one, norm_in, w_gate, w_xbc, w_step, step_bias, conv_weight, conv_bias, rates, norm_out, w_out):
    inner = HEADS * HEAD_DIM
    normed = rms_rows(columns_one.astype(jnp.float32), norm_in).astype(jnp.bfloat16)
    gate = jnp.dot(normed, w_gate, preferred_element_type=jnp.float32).astype(jnp.bfloat16)
    xbc = jnp.dot(normed, w_xbc, preferred_element_type=jnp.float32).astype(jnp.bfloat16)
    step_raw = jnp.dot(normed, w_step, preferred_element_type=jnp.float32)
    width = xbc.shape[1]
    padded = jnp.concatenate([jnp.zeros((CONV - 1, width), jnp.float32), xbc.astype(jnp.float32)], axis=0)
    conv = conv_bias + conv_weight[0] * padded[0:LEN]
    for offset in range(1, CONV):
        conv = conv + conv_weight[offset] * padded[offset:offset + LEN]
    act = jax.nn.silu(conv).astype(jnp.bfloat16)
    count = LEN // BLOCK
    xs = act[:, :inner].reshape(count, BLOCK, HEADS, HEAD_DIM)
    bm = act[:, inner:inner + STATE].reshape(count, BLOCK, STATE)
    cm = act[:, inner + STATE:].reshape(count, BLOCK, STATE)
    steps_dt = jax.nn.softplus(step_raw + step_bias)
    decay = -rates * steps_dt * gaps_one[:, None]
    steps_dt = steps_dt.reshape(count, BLOCK, HEADS)
    decay = decay.reshape(count, BLOCK, HEADS)
    rows = lax.broadcasted_iota(jnp.int32, (BLOCK, BLOCK), 0)
    cols = lax.broadcasted_iota(jnp.int32, (BLOCK, BLOCK), 1)

    def advance(state, block):
        cx, cb, cc, cdt, cda = block
        cs = jnp.cumsum(cda, axis=0)
        scores = jnp.dot(cc, cb.T, preferred_element_type=jnp.float32)
        trail = cs.T
        diff = trail[:, :, None] - trail[:, None, :]
        factor = jnp.exp(jnp.where((rows >= cols)[None], diff, -jnp.inf))
        mix = (scores[None] * factor * cdt.T[:, None, :]).astype(jnp.bfloat16)
        y_in = jnp.einsum('hts,shp->thp', mix.astype(jnp.float32), cx.astype(jnp.float32))
        rounded_state = lax.optimization_barrier(state.astype(jnp.bfloat16)).astype(jnp.float32)
        picked = jnp.einsum('tn,hpn->thp', cc.astype(jnp.float32), rounded_state)
        y_state = jnp.exp(cs)[:, :, None] * picked
        weighted = ((jnp.exp(cs[-1][None, :] - cs) * cdt)[:, :, None] * cx.astype(jnp.float32)).astype(jnp.bfloat16)
        block_state = jnp.einsum('shp,sn->hpn', weighted.astype(jnp.float32), cb.astype(jnp.float32))
        state = jnp.exp(cs[-1])[:, None, None] * state + block_state
        return (state, y_in + y_state)
    start_state = jnp.zeros((HEADS, HEAD_DIM, STATE), jnp.float32)
    final_state, outputs = lax.scan(advance, start_state, (xs, bm, cm, steps_dt, decay))
    y = outputs.reshape(LEN, inner)
    gated = y * jax.nn.silu(gate.astype(jnp.float32))
    out_normed = rms_rows(gated, norm_out).astype(jnp.bfloat16)
    return jnp.dot(out_normed, w_out, preferred_element_type=jnp.float32).astype(jnp.bfloat16)

def reference(columns, gaps, norm_in, w_gate, w_xbc, w_step, step_bias, conv_weight, conv_bias, rates, norm_out, w_out):

    def one_history(paired):
        return history(paired[0], paired[1], norm_in, w_gate, w_xbc, w_step, step_bias, conv_weight, conv_bias, rates, norm_out, w_out)
    return lax.map(one_history, (columns, gaps))
```

```python
import functools

import jax
import jax.numpy as jnp
from jax import lax
from jax.experimental import pallas as pl
from jax.experimental.pallas import tpu as pltpu
from jax.sharding import PartitionSpec as P

MESH = pl.DeviceIdType.MESH
epsilon = 1e-05
LOG2E = 1.4426950408889634
HALO = 16
CHUNK = 256
EXTRA = 16


def silu(v):
    half = 0.5 * v
    return half + half * jnp.tanh(half)


def split(v):
    hi = v.astype(jnp.bfloat16)
    return hi, (v - hi.astype(jnp.float32)).astype(jnp.bfloat16)


def dot(a, b):
    return jnp.dot(a, b, preferred_element_type=jnp.float32)


def kernel(
    tables,
    seqs,
    columns,
    gaps_h,
    norm_in_h,
    w_gate_h,
    w_xbc_h,
    w_step_h,
    step_bias_h,
    conv_weight_h,
    conv_bias_h,
    rates_h,
    norm_out_h,
    w_out_h,
    out,
    gaps,
    norm_in,
    w_gate,
    w_xbc,
    w_step,
    step_bias,
    conv_weight,
    conv_bias,
    rates,
    norm_out,
    w_out,
    cols,
    xb,
    xs,
    y_in,
    ecs,
    gate,
    states,
    decays,
    pair_state,
    pair_decay,
    middle,
    entering,
    part_send,
    part_recv,
    chain_send,
    chain_recv,
    share_send,
    load_sem,
    own_sem,
    all_send,
    all_recv,
    halo_send,
    halo_recv,
    psend,
    precv,
    csend,
    crecv,
    ssend,
    srecv,
):
    s = lax.axis_index("seq")
    t = lax.axis_index("table")
    core = lax.rem(s, 2)
    pair = s // 2
    pairs = seqs // 2
    partner = s + 1 - 2 * core
    length = gaps.shape[1]
    inner = w_gate.shape[1]
    heads = rates.shape[0]
    head_dim = inner // heads
    state = (w_xbc.shape[1] - inner) // 2
    taps = conv_weight.shape[0]
    chunks = inner // CHUNK
    half = chunks // 2
    per = CHUNK // head_dim

    sources = (w_xbc_h, w_step_h, norm_in_h, conv_weight_h, conv_bias_h, gaps_h)
    sources += (rates_h, step_bias_h, w_gate_h, norm_out_h, w_out_h)
    places = (w_xbc, w_step, norm_in, conv_weight, conv_bias, gaps)
    places += (rates, step_bias, w_gate, norm_out, w_out)
    loads = [
        pltpu.make_async_copy(a, b, load_sem.at[i])
        for i, (a, b) in enumerate(zip(sources, places))
    ]
    own = pltpu.make_async_copy(columns.at[t], cols.at[t, pl.ds(HALO, length)], own_sem)

    barrier = pltpu.get_barrier_semaphore()

    def greet(where):
        pl.semaphore_signal(barrier, inc=1, device_id=where, device_id_type=MESH)

    for off in range(1, tables):
        greet((s, lax.rem(t + off, tables)))
    greet((partner, t))

    @pl.when(s > 0)
    def _():
        for h in range(tables):
            greet((s - 1, h))

    @pl.when(s < seqs - 1)
    def _():
        for h in range(tables):
            greet((s + 1, h))

    @pl.when(pair > 0)
    def _():
        greet((s - 2, t))

    @pl.when(pair < pairs - 1)
    def _():
        greet((s + 2, t))

    own.start()
    for load in loads:
        load.start()

    @pl.when(s == 0)
    def _():
        for h in range(tables):
            cols[h, 0:HALO, :] = jnp.zeros((HALO, cols.shape[2]), cols.dtype)

    def count(held):
        return jnp.where(held, 1, 0)

    pl.semaphore_wait(
        barrier,
        tables
        + tables * (count(s > 0) + count(s < seqs - 1))
        + count(pair > 0)
        + count(pair < pairs - 1),
    )

    def across(peer, sender):
        return pltpu.make_async_remote_copy(
            src_ref=columns.at[peer],
            dst_ref=cols.at[sender, pl.ds(HALO, length)],
            send_sem=all_send.at[peer],
            recv_sem=all_recv.at[sender],
            device_id=(s, peer),
            device_id_type=MESH,
        )

    def rim(target, peer, sender):
        return pltpu.make_async_remote_copy(
            src_ref=columns.at[peer, pl.ds(length - HALO, HALO)],
            dst_ref=cols.at[sender, pl.ds(0, HALO)],
            send_sem=halo_send.at[peer],
            recv_sem=halo_recv.at[sender],
            device_id=(target, peer),
            device_id_type=MESH,
        )

    peers = [lax.rem(t + off, tables) for off in range(1, tables)]
    for peer in peers:
        across(peer, t).start()

    @pl.when(s < seqs - 1)
    def _():
        for h in range(tables):
            rim(s + 1, h, t).start()

    lane = lax.broadcasted_iota(jnp.int32, (heads, inner), 1) // head_dim
    head = lax.broadcasted_iota(jnp.int32, (heads, inner), 0)
    spread = jnp.where(lane == head, 1.0, 0.0).astype(jnp.bfloat16)
    before = lax.broadcasted_iota(jnp.int32, (length, length), 0)
    after = lax.broadcasted_iota(jnp.int32, (length, length), 1)
    upper = jnp.where(before <= after, 1.0, 0.0).astype(jnp.bfloat16)
    q = length // 2
    keep = lax.broadcasted_iota(jnp.int32, (q, q), 0) >= lax.broadcasted_iota(
        jnp.int32, (q, q), 1
    )
    low = lax.broadcasted_iota(jnp.int32, (length, 2 * head_dim), 1) < head_dim

    def expand(v):
        hi, lo = split(v)
        return dot(hi, spread) + dot(lo, spread)

    for load in loads[:8]:
        load.wait()
    own.wait()
    for peer in peers:
        across(peer, peer).wait_recv()

    @pl.when(s > 0)
    def _():
        for h in range(tables):
            rim(s, h, h).wait_recv()

    u = jnp.concatenate([cols[h] for h in range(tables)], axis=1).astype(jnp.float32)
    scale = lax.rsqrt(jnp.mean(u * u, axis=-1, keepdims=True) + epsilon)
    normed = (u * scale * norm_in[...][None, :]).astype(jnp.bfloat16)
    main = normed[HALO:]

    step_raw = dot(main, w_step[...])
    xb[...] = dot(normed, w_xbc[...]).astype(jnp.bfloat16).astype(jnp.float32)
    raw = step_raw.T + step_bias[...][:, None]
    dt = jnp.maximum(raw, 0.0) + jnp.log1p(jnp.exp(-jnp.abs(raw)))
    da = -rates[...][:, None] * dt * gaps[...]
    d1 = da.astype(jnp.bfloat16)
    left = da - d1.astype(jnp.float32)
    d2, d3 = split(left)
    cs = dot(d1, upper) + (dot(d2, upper) + dot(d3, upper))
    last = cs[:, length - 1 : length]
    ecs[...] = expand(jnp.exp(cs).T)
    weight = expand((jnp.exp(last - cs) * dt).T)
    cs2 = cs * LOG2E
    cs2t = cs2.T
    row2 = jnp.where(dt > 0.0, cs2 - jnp.log(dt) * LOG2E, 3e38)

    def conv(start, width):
        total = conv_bias[start : start + width][None, :]
        for k in range(taps):
            total = total + conv_weight[k : k + 1, start : start + width] * xb[
                pl.ds(HALO - taps + 1 + k, length), start : start + width
            ]
        return silu(total)

    bt = conv(inner, state).T.astype(jnp.bfloat16)
    cm = conv(inner + state, state).astype(jnp.bfloat16)

    for k in range(chunks):
        x = conv(k * CHUNK, CHUNK).astype(jnp.bfloat16)
        xs[k] = x
        cut = slice(k * CHUNK, (k + 1) * CHUNK)
        weighted = (weight[:, cut] * x.astype(jnp.float32)).astype(jnp.bfloat16)
        states[k] = dot(bt, weighted)
        decays[k] = jnp.broadcast_to(ecs[length - 1 : length, cut], (8, CHUNK))

    def to_partner(j):
        return pltpu.make_async_remote_copy(
            src_ref=part_send.at[j],
            dst_ref=part_recv.at[j],
            send_sem=psend.at[j],
            recv_sem=precv.at[j],
            device_id=(partner, t),
            device_id_type=MESH,
        )

    rows = lax.broadcasted_iota(jnp.int32, (EXTRA, CHUNK), 0)
    for j in range(half):
        k = half * (1 - core) + j
        hi, lo = split(decays[k][0:1])
        part_send[j, 0:state, :] = states[k].astype(jnp.bfloat16)
        part_send[j, state : state + EXTRA, :] = jnp.where(
            rows == 0, hi.astype(jnp.float32), jnp.where(rows == 1, lo.astype(jnp.float32), 0.0)
        ).astype(jnp.bfloat16)
        to_partner(j).start()

    scores = dot(cm, bt)
    top = jnp.where(keep, scores[:q, :q], 0.0)
    side = scores[q:, :q]
    end = jnp.where(keep, scores[q:, q:], 0.0)

    def mix_of(h):
        c0, c1 = cs2t[:q, h : h + 1], cs2t[q:, h : h + 1]
        r0, r1 = row2[h : h + 1, :q], row2[h : h + 1, q:]
        m0 = jnp.where(keep, top * jnp.exp2(c0 - r0), 0.0).astype(jnp.bfloat16)
        m1 = (side * jnp.exp2(c1 - r0)).astype(jnp.bfloat16)
        m2 = jnp.where(keep, end * jnp.exp2(c1 - r1), 0.0).astype(jnp.bfloat16)
        return m0, jnp.concatenate([m1, m2], axis=1)

    def intra(k):
        for p in range(per // 2):
            pairx = xs[k, :, p * 2 * head_dim : (p + 1) * 2 * head_dim]
            got = []
            for e in range(2):
                m0, m1 = mix_of(k * per + 2 * p + e)
                got.append(jnp.concatenate([dot(m0, pairx[:q]), dot(m1, pairx)], axis=0))
            y_in[k, :, p * 2 * head_dim : (p + 1) * 2 * head_dim] = jnp.where(low, got[0], got[1])

    def chain(j):
        return pltpu.make_async_remote_copy(
            src_ref=chain_send.at[j],
            dst_ref=chain_recv.at[j],
            send_sem=csend.at[j],
            recv_sem=crecv.at[j],
            device_id=(s + 2, t),
            device_id_type=MESH,
        )

    def share(j, k):
        return pltpu.make_async_remote_copy(
            src_ref=share_send.at[j],
            dst_ref=entering.at[k],
            send_sem=ssend.at[j],
            recv_sem=srecv.at[j],
            device_id=(partner, t),
            device_id_type=MESH,
        )

    odd = core == 1

    def join():
        for j in range(half):
            k = half * core + j
            to_partner(j).wait_recv()
            theirs = part_recv[j, 0:state, :].astype(jnp.float32)
            tail = part_recv[j, state : state + EXTRA, :].astype(jnp.float32)
            their_decay = tail[0:1] + tail[1:2]
            mine = states[k]
            my_decay = decays[k][0:1]
            first = jnp.where(odd, theirs, mine)
            second = jnp.where(odd, mine, theirs)
            first_decay = jnp.where(odd, their_decay, my_decay)
            second_decay = jnp.where(odd, my_decay, their_decay)
            pair_state[j] = second_decay * first + second
            pair_decay[j] = jnp.broadcast_to(second_decay * first_decay, (8, CHUNK))
            middle[j] = first
            decays[k] = jnp.broadcast_to(first_decay, (8, CHUNK))

    def step(entry):
        for j in range(half):
            k = half * core + j
            if entry:
                chain(j).wait_recv()
                came = chain_recv[j].astype(jnp.float32)
                leaving = pair_decay[j][0:1] * came + pair_state[j]
                between = decays[k][0:1] * came + middle[j]
            else:
                came = jnp.zeros((state, CHUNK), jnp.float32)
                leaving = pair_state[j]
                between = middle[j]

            @pl.when(pair < pairs - 1)
            def _():
                chain_send[j] = leaving.astype(jnp.bfloat16)
                chain(j).start()

            share_send[j] = jnp.where(odd, came, between).astype(jnp.bfloat16)
            share(j, k).start()
            entering[k] = jnp.where(odd, between, came).astype(jnp.bfloat16)

    for k in range(chunks):
        intra(k)
        if k == 0:
            join()

            @pl.when(pair == 0)
            def _():
                step(False)

        elif k < chunks - 1:

            @pl.when(pair == k)
            def _():
                step(True)

    loads[8].wait()
    gate[...] = silu(dot(main, w_gate[...]).astype(jnp.bfloat16).astype(jnp.float32))

    @pl.when(pair >= chunks - 1)
    def _():
        step(True)

    for j in range(half):
        share(j, half * (1 - core) + j).wait_recv()
    loads[9].wait()
    loads[10].wait()

    square = jnp.zeros((length, 1), jnp.float32)
    for k in range(chunks):
        cut = slice(k * CHUNK, (k + 1) * CHUNK)
        y = y_in[k] + ecs[:, cut] * dot(cm, entering[k])
        g = y * gate[:, cut]
        square = square + jnp.sum(g * g, axis=-1, keepdims=True)
        y_in[k] = g
    scale = lax.rsqrt(square / inner + epsilon)
    gathered = [
        (y_in[k] * scale * norm_out[k * CHUNK : (k + 1) * CHUNK][None, :]).astype(jnp.bfloat16)
        for k in range(chunks)
    ]
    out[...] = dot(jnp.concatenate(gathered, axis=1), w_out[...]).astype(out.dtype)

    for peer in peers:
        across(peer, t).wait_send()

    @pl.when(s < seqs - 1)
    def _():
        for h in range(tables):
            rim(s + 1, h, t).wait_send()

    for j in range(half):
        to_partner(j).wait_send()
        share(j, half * core + j).wait_send()

    @pl.when(pair < pairs - 1)
    def _():
        for j in range(half):
            chain(j).wait_send()


def local(tables, seqs, *args):
    columns, gaps, norm_in, w_gate, w_xbc, w_step = args[:6]
    step_bias, conv_weight, conv_bias, rates, norm_out, w_out = args[6:]
    length = columns.shape[1]
    inner = w_gate.shape[1]
    state = (w_xbc.shape[1] - inner) // 2
    chunks = inner // CHUNK
    half = chunks // 2
    f32, bf16 = jnp.float32, jnp.bfloat16
    dma = pltpu.SemaphoreType.DMA
    scratch = [pltpu.VMEM(a.shape, a.dtype) for a in args[1:]]
    scratch += [
        pltpu.VMEM((tables, HALO + length, columns.shape[2]), bf16),
        pltpu.VMEM((HALO + length, w_xbc.shape[1]), f32),
        pltpu.VMEM((chunks, length, CHUNK), bf16),
        pltpu.VMEM((chunks, length, CHUNK), f32),
        pltpu.VMEM((length, inner), f32),
        pltpu.VMEM((length, inner), f32),
        pltpu.VMEM((chunks, state, CHUNK), f32),
        pltpu.VMEM((chunks, 8, CHUNK), f32),
        pltpu.VMEM((half, state, CHUNK), f32),
        pltpu.VMEM((half, 8, CHUNK), f32),
        pltpu.VMEM((half, state, CHUNK), f32),
        pltpu.VMEM((chunks, state, CHUNK), bf16),
        pltpu.VMEM((half, state + EXTRA, CHUNK), bf16),
        pltpu.VMEM((half, state + EXTRA, CHUNK), bf16),
        pltpu.VMEM((half, state, CHUNK), bf16),
        pltpu.VMEM((half, state, CHUNK), bf16),
        pltpu.VMEM((half, state, CHUNK), bf16),
        dma((11,)),
        dma(()),
        dma((tables,)),
        dma((tables,)),
        dma((tables,)),
        dma((tables,)),
        dma((half,)),
        dma((half,)),
        dma((half,)),
        dma((half,)),
        dma((half,)),
        dma((half,)),
    ]
    got = pl.pallas_call(
        functools.partial(kernel, tables, seqs),
        out_shape=jax.ShapeDtypeStruct((length, w_out.shape[1]), bf16),
        in_specs=[pl.BlockSpec(memory_space=pl.ANY)] * len(args),
        out_specs=pl.BlockSpec(memory_space=pltpu.VMEM),
        scratch_shapes=scratch,
        compiler_params=pltpu.CompilerParams(
            collective_id=0, has_side_effects=True, vmem_limit_bytes=48 * 2**20
        ),
        cost_estimate=pl.CostEstimate(
            flops=2 * 10**9, bytes_accessed=4 * 10**6, transcendentals=2 * 10**6
        ),
    )(*args)
    return got[None]


def solution(mesh):
    in_specs = (P(None, "seq", "table"), P("table", "seq")) + (P(),) * 10
    return jax.shard_map(
        functools.partial(local, mesh.shape["table"], mesh.shape["seq"]),
        mesh=mesh,
        in_specs=in_specs,
        out_specs=P("table", "seq", None),
        check_vma=False,
    )
```

```python
import functools

import jax
import jax.numpy as jnp
from jax import lax
from jax.experimental import pallas as pl
from jax.experimental.pallas import tpu as pltpu
from jax.sharding import PartitionSpec as P

MESH = pl.DeviceIdType.MESH
epsilon = 1e-05
LOG2E = 1.4426950408889634
HALO = 16
CHUNK = 256
PIECE = 128
EXTRA = 16


def silu(v):
    half = 0.5 * v
    return half + half * jnp.tanh(half)


def split(v):
    hi = v.astype(jnp.bfloat16)
    return hi, (v - hi.astype(jnp.float32)).astype(jnp.bfloat16)


def dot(a, b):
    return jnp.dot(a, b, preferred_element_type=jnp.float32)


def kernel(
    tables,
    seqs,
    columns,
    gaps_h,
    norm_in_h,
    w_gate_h,
    w_xbc_h,
    w_step_h,
    step_bias_h,
    conv_weight_h,
    conv_bias_h,
    rates_h,
    norm_out_h,
    w_out_h,
    out,
    gaps,
    norm_in,
    w_gate,
    w_xbc,
    w_step,
    step_bias,
    conv_weight,
    conv_bias,
    rates,
    norm_out,
    w_out,
    cols,
    xb,
    xs,
    y_in,
    ecs,
    gate,
    states,
    decays,
    pair_state,
    pair_decay,
    first_decays,
    middle,
    entering,
    part_send,
    part_recv,
    chain_send,
    chain_recv,
    share_send,
    weight,
    bias_row,
    out_row,
    load_sem,
    own_sem,
    all_send,
    all_recv,
    halo_send,
    halo_recv,
    psend,
    precv,
    csend,
    crecv,
    ssend,
    srecv,
):
    s = lax.axis_index("seq")
    t = lax.axis_index("table")
    core = lax.rem(s, 2)
    pair = s // 2
    pairs = seqs // 2
    partner = s + 1 - 2 * core
    length = gaps.shape[1]
    inner = w_gate.shape[1]
    heads = rates.shape[0]
    pieces = CHUNK // PIECE
    head_dim = inner // heads
    state = (w_xbc.shape[1] - inner) // 2
    taps = conv_weight.shape[0]
    chunks = inner // CHUNK
    half = chunks // 2
    per = CHUNK // head_dim

    sources = (w_xbc_h, w_step_h, norm_in_h, conv_weight_h, conv_bias_h, gaps_h)
    sources += (rates_h, step_bias_h, w_gate_h, norm_out_h, w_out_h)
    places = (w_xbc, w_step, norm_in, conv_weight, conv_bias, gaps)
    places += (rates, step_bias, w_gate, norm_out, w_out)
    loads = [
        pltpu.make_async_copy(a, b, load_sem.at[i])
        for i, (a, b) in enumerate(zip(sources, places))
    ]
    own = pltpu.make_async_copy(columns.at[t], cols.at[t, pl.ds(HALO, length)], own_sem)

    barrier = pltpu.get_barrier_semaphore()

    def greet(where):
        pl.semaphore_signal(barrier, inc=1, device_id=where, device_id_type=MESH)

    for off in range(1, tables):
        greet((s, lax.rem(t + off, tables)))
    greet((partner, t))

    @pl.when(s > 0)
    def _():
        for h in range(tables):
            greet((s - 1, h))

    @pl.when(s < seqs - 1)
    def _():
        for h in range(tables):
            greet((s + 1, h))

    @pl.when(pair > 0)
    def _():
        greet((s - 2, t))

    @pl.when(pair < pairs - 1)
    def _():
        greet((s + 2, t))

    own.start()
    for load in loads:
        load.start()

    @pl.when(s == 0)
    def _():
        for h in range(tables):
            cols[h, 0:HALO, :] = jnp.zeros((HALO, cols.shape[2]), cols.dtype)

    def count(held):
        return jnp.where(held, 1, 0)

    pl.semaphore_wait(
        barrier,
        tables
        + tables * (count(s > 0) + count(s < seqs - 1))
        + count(pair > 0)
        + count(pair < pairs - 1),
    )

    def across(peer, sender):
        return pltpu.make_async_remote_copy(
            src_ref=columns.at[peer],
            dst_ref=cols.at[sender, pl.ds(HALO, length)],
            send_sem=all_send.at[peer],
            recv_sem=all_recv.at[sender],
            device_id=(s, peer),
            device_id_type=MESH,
        )

    def rim(target, peer, sender):
        return pltpu.make_async_remote_copy(
            src_ref=columns.at[peer, pl.ds(length - HALO, HALO)],
            dst_ref=cols.at[sender, pl.ds(0, HALO)],
            send_sem=halo_send.at[peer],
            recv_sem=halo_recv.at[sender],
            device_id=(target, peer),
            device_id_type=MESH,
        )

    peers = [lax.rem(t + off, tables) for off in range(1, tables)]
    for peer in peers:
        across(peer, t).start()

    @pl.when(s < seqs - 1)
    def _():
        for h in range(tables):
            rim(s + 1, h, t).start()

    lane = lax.broadcasted_iota(jnp.int32, (heads, inner), 1) // head_dim
    head = lax.broadcasted_iota(jnp.int32, (heads, inner), 0)
    spread = jnp.where(lane == head, 1.0, 0.0).astype(jnp.bfloat16)
    before = lax.broadcasted_iota(jnp.int32, (length, length), 0)
    after = lax.broadcasted_iota(jnp.int32, (length, length), 1)
    upper = jnp.where(before <= after, 1.0, 0.0).astype(jnp.bfloat16)
    q = length // 2
    keep = lax.broadcasted_iota(jnp.int32, (q, q), 0) >= lax.broadcasted_iota(
        jnp.int32, (q, q), 1
    )
    low = lax.broadcasted_iota(jnp.int32, (length, 2 * head_dim), 1) < head_dim

    def expand(v):
        hi, lo = split(v)
        return dot(hi, spread) + dot(lo, spread)

    for load in loads[:8]:
        load.wait()
    own.wait()
    for peer in peers:
        across(peer, peer).wait_recv()

    @pl.when(s > 0)
    def _():
        for h in range(tables):
            rim(s, h, h).wait_recv()

    u = jnp.concatenate([cols[h] for h in range(tables)], axis=1).astype(jnp.float32)
    scale = lax.rsqrt(jnp.mean(u * u, axis=-1, keepdims=True) + epsilon)
    normed = (u * scale * norm_in[...][None, :]).astype(jnp.bfloat16)
    main = normed[HALO:]

    step_raw = lax.dot_general(
        w_step[...], main, (((1,), (1,)), ((), ())), preferred_element_type=jnp.float32
    )
    xb[...] = dot(normed, w_xbc[...]).astype(jnp.bfloat16).astype(jnp.float32)
    raw = step_raw + step_bias[...][:, None]
    dt = jnp.maximum(raw, 0.0) + jnp.log1p(jnp.exp(-jnp.abs(raw)))
    da = -rates[...][:, None] * dt * gaps[...]
    d1 = da.astype(jnp.bfloat16)
    left = da - d1.astype(jnp.float32)
    d2, d3 = split(left)
    cs = dot(d1, upper) + (dot(d2, upper) + dot(d3, upper))
    last = cs[:, length - 1 : length]
    grown = expand(jnp.exp(cs).T)
    faded = expand((jnp.exp(last - cs) * dt).T)
    for k in range(chunks):
        cut = slice(k * CHUNK, (k + 1) * CHUNK)
        ecs[k] = grown[:, cut]
        weight[k] = faded[:, cut]
        decays[k] = jnp.broadcast_to(grown[length - 1 : length, cut], (8, CHUNK))
    bias_row[...] = conv_bias[...][None, :]
    cs2 = cs * LOG2E
    cs2t = cs2.T
    row2 = jnp.where(dt > 0.0, cs2 - jnp.log(dt) * LOG2E, 3e38)

    def conv(start, width):
        lanes = pl.ds(start, width)
        total = bias_row[:, lanes]
        for k in range(taps):
            total = total + conv_weight[pl.ds(k, 1), lanes] * xb[
                pl.ds(HALO - taps + 1 + k, length), lanes
            ]
        return silu(total)

    def to_partner(i):
        return pltpu.make_async_remote_copy(
            src_ref=part_send.at[i],
            dst_ref=part_recv.at[i],
            send_sem=psend.at[i],
            recv_sem=precv.at[i],
            device_id=(partner, t),
            device_id_type=MESH,
        )

    rows = lax.broadcasted_iota(jnp.int32, (EXTRA, PIECE), 0)
    bt = conv(inner, state).T.astype(jnp.bfloat16)
    cm = conv(inner + state, state).astype(jnp.bfloat16)
    for j in range(chunks):
        k = lax.rem(half * (1 - core) + j, chunks)
        x = conv(pl.multiple_of(k * CHUNK, CHUNK), CHUNK).astype(jnp.bfloat16)
        xs[k] = x
        made = dot(bt, (weight[k] * x.astype(jnp.float32)).astype(jnp.bfloat16))
        if j >= half:
            states[k] = made
            continue
        hi, lo = split(decays[k][0:1])
        hi, lo = hi.astype(jnp.float32), lo.astype(jnp.float32)
        for e in range(pieces):
            cut = slice(e * PIECE, (e + 1) * PIECE)
            tail = jnp.where(rows == 0, hi[:, cut], jnp.where(rows == 1, lo[:, cut], 0.0))
            part_send[j * pieces + e, 0:state, :] = made[:, cut].astype(jnp.bfloat16)
            part_send[j * pieces + e, state : state + EXTRA, :] = tail.astype(jnp.bfloat16)
            to_partner(j * pieces + e).start()

    scores = dot(cm, bt)
    top = jnp.where(keep, scores[:q, :q], 0.0)
    side = scores[q:, :q]
    end = jnp.where(keep, scores[q:, q:], 0.0)

    def mix_of(h):
        c0, c1 = cs2t[:q, h : h + 1], cs2t[q:, h : h + 1]
        r0, r1 = row2[h : h + 1, :q], row2[h : h + 1, q:]
        m0 = jnp.where(keep, top * jnp.exp2(c0 - r0), 0.0).astype(jnp.bfloat16)
        m1 = (side * jnp.exp2(c1 - r0)).astype(jnp.bfloat16)
        m2 = jnp.where(keep, end * jnp.exp2(c1 - r1), 0.0).astype(jnp.bfloat16)
        return m0, jnp.concatenate([m1, m2], axis=1)

    def intra(k):
        for p in range(per // 2):
            pairx = xs[k, :, p * 2 * head_dim : (p + 1) * 2 * head_dim]
            got = []
            for e in range(2):
                m0, m1 = mix_of(k * per + 2 * p + e)
                got.append(jnp.concatenate([dot(m0, pairx[:q]), dot(m1, pairx)], axis=0))
            y_in[k, :, p * 2 * head_dim : (p + 1) * 2 * head_dim] = jnp.where(low, got[0], got[1])

    def chain(i):
        return pltpu.make_async_remote_copy(
            src_ref=chain_send.at[i],
            dst_ref=chain_recv.at[i],
            send_sem=csend.at[i],
            recv_sem=crecv.at[i],
            device_id=(s + 2, t),
            device_id_type=MESH,
        )

    def share(i, where):
        return pltpu.make_async_remote_copy(
            src_ref=share_send.at[i],
            dst_ref=entering.at[where * half * pieces + i],
            send_sem=ssend.at[i],
            recv_sem=srecv.at[i],
            device_id=(partner, t),
            device_id_type=MESH,
        )

    odd = core == 1

    def join(i):
        k, e = half * core + i // pieces, i % pieces
        cut = slice(e * PIECE, (e + 1) * PIECE)
        to_partner(i).wait_recv()
        theirs = part_recv[i, 0:state, :].astype(jnp.float32)
        tail = part_recv[i, state : state + EXTRA, :].astype(jnp.float32)
        their_decay = tail[0:1] + tail[1:2]
        mine = states[k][:, cut]
        my_decay = decays[k][0:1, cut]
        first = jnp.where(odd, theirs, mine)
        second = jnp.where(odd, mine, theirs)
        first_decay = jnp.where(odd, their_decay, my_decay)
        second_decay = jnp.where(odd, my_decay, their_decay)
        total = second_decay * first + second

        @pl.when((pair == 0) & (pairs > 1))
        def _():
            chain_send[i] = total.astype(jnp.bfloat16)
            chain(i).start()

        pair_state[i] = total
        pair_decay[i] = jnp.broadcast_to(second_decay * first_decay, (8, PIECE))
        middle[i] = first
        first_decays[i] = jnp.broadcast_to(first_decay, (8, PIECE))

    def step(i, entry):
        place = core * half * pieces + i
        if entry:
            chain(i).wait_recv()
            came = chain_recv[i].astype(jnp.float32)

            @pl.when(pair < pairs - 1)
            def _():
                leaving = pair_decay[i][0:1] * came + pair_state[i]
                chain_send[i] = leaving.astype(jnp.bfloat16)
                chain(i).start()

            between = first_decays[i][0:1] * came + middle[i]
        else:
            came = jnp.zeros((state, PIECE), jnp.float32)
            between = middle[i]
        share_send[i] = jnp.where(odd, came, between).astype(jnp.bfloat16)
        share(i, core).start()
        entering[place] = jnp.where(odd, between, came).astype(jnp.bfloat16)

    for k in range(chunks):
        intra(k)
        if k == 0:
            for i in range(half * pieces):
                join(i)

            @pl.when(pair == 0)
            def _():
                for i in range(half * pieces):
                    step(i, False)

        elif k < chunks - 1:

            @pl.when(pair == k)
            def _():
                for i in range(half * pieces):
                    step(i, True)

    loads[8].wait()
    gated = silu(dot(main, w_gate[...]).astype(jnp.bfloat16).astype(jnp.float32))
    for k in range(chunks):
        gate[k] = gated[:, k * CHUNK : (k + 1) * CHUNK]
    loads[9].wait()
    loads[10].wait()
    out_row[...] = norm_out[...][None, :]

    def finish(k, square, total):
        entry = jnp.concatenate([entering[k * pieces + e] for e in range(pieces)], axis=1)
        start = pl.multiple_of(k * CHUNK, CHUNK)
        g = (y_in[k] + ecs[k] * dot(cm, entry)) * gate[k]
        square = square + jnp.sum(g * g, axis=-1, keepdims=True)
        scaled = (g * out_row[:, pl.ds(start, CHUNK)]).astype(jnp.bfloat16)
        return square, total + dot(scaled, w_out[pl.ds(start, CHUNK), :])

    square = jnp.zeros((length, 1), jnp.float32)
    total = jnp.zeros((length, out.shape[1]), jnp.float32)
    for j in range(half):

        @pl.when(pair >= chunks - 1)
        def _():
            for e in range(pieces):
                step(j * pieces + e, True)

        square, total = finish(half * core + j, square, total)
    for j in range(half):
        for e in range(pieces):
            share(j * pieces + e, 1 - core).wait_recv()
        square, total = finish(half * (1 - core) + j, square, total)
    out[...] = (total * lax.rsqrt(square / inner + epsilon)).astype(out.dtype)

    for peer in peers:
        across(peer, t).wait_send()

    @pl.when(s < seqs - 1)
    def _():
        for h in range(tables):
            rim(s + 1, h, t).wait_send()

    for i in range(half * pieces):
        to_partner(i).wait_send()
        share(i, core).wait_send()

    @pl.when(pair < pairs - 1)
    def _():
        for i in range(half * pieces):
            chain(i).wait_send()


def local(tables, seqs, *args):
    args = args[:5] + (args[5].T,) + args[6:]
    columns, gaps, norm_in, w_gate, w_xbc, w_step = args[:6]
    step_bias, conv_weight, conv_bias, rates, norm_out, w_out = args[6:]
    length = columns.shape[1]
    inner = w_gate.shape[1]
    state = (w_xbc.shape[1] - inner) // 2
    chunks = inner // CHUNK
    count = chunks // 2 * (CHUNK // PIECE)
    f32, bf16 = jnp.float32, jnp.bfloat16
    dma = pltpu.SemaphoreType.DMA
    scratch = [pltpu.VMEM(a.shape, a.dtype) for a in args[1:]]
    scratch += [
        pltpu.VMEM((tables, HALO + length, columns.shape[2]), bf16),
        pltpu.VMEM((HALO + length, w_xbc.shape[1]), f32),
        pltpu.VMEM((chunks, length, CHUNK), bf16),
        pltpu.VMEM((chunks, length, CHUNK), f32),
        pltpu.VMEM((chunks, length, CHUNK), f32),
        pltpu.VMEM((chunks, length, CHUNK), f32),
        pltpu.VMEM((chunks, state, CHUNK), f32),
        pltpu.VMEM((chunks, 8, CHUNK), f32),
        pltpu.VMEM((count, state, PIECE), f32),
        pltpu.VMEM((count, 8, PIECE), f32),
        pltpu.VMEM((count, 8, PIECE), f32),
        pltpu.VMEM((count, state, PIECE), f32),
        pltpu.VMEM((2 * count, state, PIECE), bf16),
        pltpu.VMEM((count, state + EXTRA, PIECE), bf16),
        pltpu.VMEM((count, state + EXTRA, PIECE), bf16),
        pltpu.VMEM((count, state, PIECE), bf16),
        pltpu.VMEM((count, state, PIECE), bf16),
        pltpu.VMEM((count, state, PIECE), bf16),
        pltpu.VMEM((chunks, length, CHUNK), f32),
        pltpu.VMEM((1, w_xbc.shape[1]), f32),
        pltpu.VMEM((1, inner), f32),
        dma((11,)),
        dma(()),
        dma((tables,)),
        dma((tables,)),
        dma((tables,)),
        dma((tables,)),
        dma((count,)),
        dma((count,)),
        dma((count,)),
        dma((count,)),
        dma((count,)),
        dma((count,)),
    ]
    got = pl.pallas_call(
        functools.partial(kernel, tables, seqs),
        out_shape=jax.ShapeDtypeStruct((length, w_out.shape[1]), bf16),
        in_specs=[pl.BlockSpec(memory_space=pltpu.HBM)] * len(args),
        out_specs=pl.BlockSpec(memory_space=pltpu.VMEM),
        scratch_shapes=scratch,
        compiler_params=pltpu.CompilerParams(
            collective_id=0, has_side_effects=True, vmem_limit_bytes=63 * 2**20
        ),
        cost_estimate=pl.CostEstimate(
            flops=2 * 10**9, bytes_accessed=4 * 10**6, transcendentals=2 * 10**6
        ),
    )(*args)
    return got[None]


def solution(mesh):
    in_specs = (P(None, "seq", "table"), P("table", "seq")) + (P(),) * 10
    return jax.shard_map(
        functools.partial(local, mesh.shape["table"], mesh.shape["seq"]),
        mesh=mesh,
        in_specs=in_specs,
        out_specs=P("table", "seq", None),
        check_vma=False,
    )
```

```python
import functools

import jax
import jax.numpy as jnp
from jax import lax
from jax.experimental import pallas as pl
from jax.experimental.pallas import tpu as pltpu
from jax.sharding import PartitionSpec as P

MESH = pl.DeviceIdType.MESH
epsilon = 1e-05
LOG2E = 1.4426950408889634
HALO = 16
CHUNK = 256
PIECE = 128
ROWS = 64
EXTRA = 16


def silu(v):
    half = 0.5 * v
    return half + half * jnp.tanh(half)


def split(v):
    hi = v.astype(jnp.bfloat16)
    return hi, (v - hi.astype(jnp.float32)).astype(jnp.bfloat16)


def dot(a, b):
    return jnp.dot(a, b, preferred_element_type=jnp.float32)


def kernel(
    tables,
    seqs,
    columns,
    gaps_h,
    norm_in_h,
    w_gate_h,
    w_xbc_h,
    w_step_h,
    step_bias_h,
    conv_weight_h,
    conv_bias_h,
    rates_h,
    norm_out_h,
    w_out_h,
    out,
    gaps,
    norm_in,
    w_gate,
    w_xbc,
    w_step,
    step_bias,
    conv_weight,
    conv_bias,
    rates,
    norm_out,
    w_out,
    cols,
    xb,
    xs,
    y_in,
    ecs,
    gate,
    states,
    decays,
    pair_state,
    pair_decay,
    first_decays,
    middle,
    entering,
    part_send,
    part_recv,
    chain_send,
    chain_recv,
    share_send,
    spread_s,
    nm,
    bias_row,
    out_row,
    load_sem,
    own_sem,
    all_send,
    all_recv,
    halo_send,
    halo_recv,
    psend,
    precv,
    csend,
    crecv,
    ssend,
    srecv,
):
    s = lax.axis_index("seq")
    t = lax.axis_index("table")
    core = lax.rem(s, 2)
    pair = s // 2
    pairs = seqs // 2
    partner = s + 1 - 2 * core
    length = gaps.shape[1]
    inner = w_gate.shape[1]
    heads = rates.shape[0]
    pieces = CHUNK // PIECE
    head_dim = inner // heads
    state = (w_xbc.shape[1] - inner) // 2
    parts = state // ROWS
    taps = conv_weight.shape[0]
    chunks = inner // CHUNK
    half = chunks // 2
    per = CHUNK // head_dim

    sources = (w_xbc_h, w_step_h, norm_in_h, conv_weight_h, conv_bias_h, gaps_h)
    sources += (rates_h, step_bias_h, w_gate_h, norm_out_h, w_out_h)
    places = (w_xbc, w_step, norm_in, conv_weight, conv_bias, gaps)
    places += (rates, step_bias, w_gate, norm_out, w_out)
    loads = [
        pltpu.make_async_copy(a, b, load_sem.at[i])
        for i, (a, b) in enumerate(zip(sources, places))
    ]
    own = pltpu.make_async_copy(columns.at[t], cols.at[t, pl.ds(HALO, length)], own_sem)

    barrier = pltpu.get_barrier_semaphore()

    def greet(where):
        pl.semaphore_signal(barrier, inc=1, device_id=where, device_id_type=MESH)

    for off in range(1, tables):
        greet((s, lax.rem(t + off, tables)))
    greet((partner, t))

    @pl.when(s > 0)
    def _():
        for h in range(tables):
            greet((s - 1, h))

    @pl.when(s < seqs - 1)
    def _():
        for h in range(tables):
            greet((s + 1, h))

    @pl.when(pair > 0)
    def _():
        greet((s - 2, t))

    @pl.when(pair < pairs - 1)
    def _():
        greet((s + 2, t))

    own.start()
    for load in loads:
        load.start()

    @pl.when(s == 0)
    def _():
        for h in range(tables):
            cols[h, 0:HALO, :] = jnp.zeros((HALO, cols.shape[2]), cols.dtype)

    def count(held):
        return jnp.where(held, 1, 0)

    pl.semaphore_wait(
        barrier,
        tables
        + tables * (count(s > 0) + count(s < seqs - 1))
        + count(pair > 0)
        + count(pair < pairs - 1),
    )

    q = length // 2

    def across(r, peer, sender):
        return pltpu.make_async_remote_copy(
            src_ref=columns.at[peer, pl.ds(r * q, q)],
            dst_ref=cols.at[sender, pl.ds(HALO + r * q, q)],
            send_sem=all_send.at[r, peer],
            recv_sem=all_recv.at[r, sender],
            device_id=(s, peer),
            device_id_type=MESH,
        )

    def rim(target, peer, sender):
        return pltpu.make_async_remote_copy(
            src_ref=columns.at[peer, pl.ds(length - HALO, HALO)],
            dst_ref=cols.at[sender, pl.ds(0, HALO)],
            send_sem=halo_send.at[peer],
            recv_sem=halo_recv.at[sender],
            device_id=(target, peer),
            device_id_type=MESH,
        )

    peers = [lax.rem(t + off, tables) for off in range(1, tables)]
    for peer in peers:
        across(0, peer, t).start()

    @pl.when(s < seqs - 1)
    def _():
        for h in range(tables):
            rim(s + 1, h, t).start()

    for peer in peers:
        across(1, peer, t).start()

    lane = lax.broadcasted_iota(jnp.int32, (heads, inner), 1) // head_dim
    head = lax.broadcasted_iota(jnp.int32, (heads, inner), 0)
    spread_s[...] = jnp.where(lane == head, 1.0, 0.0).astype(jnp.bfloat16)
    before = lax.broadcasted_iota(jnp.int32, (length, length), 0)
    after = lax.broadcasted_iota(jnp.int32, (length, length), 1)
    upper = jnp.where(before <= after, 1.0, 0.0).astype(jnp.bfloat16)
    keep = lax.broadcasted_iota(jnp.int32, (q, q), 0) >= lax.broadcasted_iota(
        jnp.int32, (q, q), 1
    )
    low = lax.broadcasted_iota(jnp.int32, (length, 2 * head_dim), 1) < head_dim

    def expand(v, lanes):
        hi, lo = split(v)
        return dot(hi, spread_s[:, lanes]) + dot(lo, spread_s[:, lanes])

    for load in loads[:8]:
        load.wait()
    own.wait()
    bias_row[...] = conv_bias[...][None, :]

    def norm(begin, end):
        u = jnp.concatenate([cols[h, begin:end, :] for h in range(tables)], axis=1)
        u = u.astype(jnp.float32)
        scale = lax.rsqrt(jnp.mean(u * u, axis=-1, keepdims=True) + epsilon)
        nm[begin:end, :] = (u * scale * norm_in[...][None, :]).astype(jnp.bfloat16)

    def project(begin, end, lanes):
        made = dot(nm[begin:end, :], w_xbc[:, lanes])
        xb[begin:end, lanes] = made.astype(jnp.bfloat16).astype(jnp.float32)

    for peer in peers:
        across(0, peer, peer).wait_recv()

    @pl.when(s > 0)
    def _():
        for h in range(tables):
            rim(s, h, h).wait_recv()

    norm(0, HALO + q)
    project(0, HALO + q, slice(None))
    for peer in peers:
        across(1, peer, peer).wait_recv()
    norm(HALO + q, HALO + length)

    main = nm[HALO:, :]
    step_raw = lax.dot_general(
        w_step[...], main, (((1,), (1,)), ((), ())), preferred_element_type=jnp.float32
    )
    project(HALO + q, HALO + length, slice(inner, inner + 2 * state))
    raw = step_raw + step_bias[...][:, None]
    dt = jnp.maximum(raw, 0.0) + jnp.log1p(jnp.exp(-jnp.abs(raw)))
    da = -rates[...][:, None] * dt * gaps[...]
    d1 = da.astype(jnp.bfloat16)
    left = da - d1.astype(jnp.float32)
    d2, d3 = split(left)
    cs = dot(d1, upper) + (dot(d2, upper) + dot(d3, upper))
    last = cs[:, length - 1 : length]
    cst = cs.T
    faded = (jnp.exp(last - cs) * dt).T
    closing = jnp.exp(cst[length - 16 :])

    def conv(start, width):
        lanes = pl.ds(start, width)
        total = bias_row[:, lanes]
        for k in range(taps):
            total = total + conv_weight[pl.ds(k, 1), lanes] * xb[
                pl.ds(HALO - taps + 1 + k, length), lanes
            ]
        return silu(total)

    def to_partner(i):
        return pltpu.make_async_remote_copy(
            src_ref=part_send.at[i],
            dst_ref=part_recv.at[i],
            send_sem=psend.at[i],
            recv_sem=precv.at[i],
            device_id=(partner, t),
            device_id_type=MESH,
        )

    rows = lax.broadcasted_iota(jnp.int32, (EXTRA, PIECE), 0)
    bt = conv(inner, state).T.astype(jnp.bfloat16)
    for j in range(chunks):
        k = lax.rem(half * (1 - core) + j, chunks)
        start = pl.multiple_of(k * CHUNK, CHUNK)
        lanes = pl.ds(start, CHUNK)
        project(HALO + q, HALO + length, lanes)
        x = conv(start, CHUNK).astype(jnp.bfloat16)
        xs[k] = x
        weighted = expand(faded, lanes) * x.astype(jnp.float32)
        made = dot(bt, weighted.astype(jnp.bfloat16))
        decays[k] = jnp.broadcast_to(expand(closing, lanes)[15:16], (8, CHUNK))
        if j >= half:
            states[k] = made
            continue
        hi, lo = split(decays[k][0:1])
        hi, lo = hi.astype(jnp.float32), lo.astype(jnp.float32)
        for e in range(pieces):
            cut = slice(e * PIECE, (e + 1) * PIECE)
            tail = jnp.where(rows == 0, hi[:, cut], jnp.where(rows == 1, lo[:, cut], 0.0))
            part_send[j * pieces + e, 0:state, :] = made[:, cut].astype(jnp.bfloat16)
            part_send[j * pieces + e, state : state + EXTRA, :] = tail.astype(jnp.bfloat16)
            to_partner(j * pieces + e).start()

    def chain(i, r):
        return pltpu.make_async_remote_copy(
            src_ref=chain_send.at[i, pl.ds(r * ROWS, ROWS)],
            dst_ref=chain_recv.at[i, pl.ds(r * ROWS, ROWS)],
            send_sem=csend.at[i, r],
            recv_sem=crecv.at[i, r],
            device_id=(s + 2, t),
            device_id_type=MESH,
        )

    def share(i, where):
        return pltpu.make_async_remote_copy(
            src_ref=share_send.at[i],
            dst_ref=entering.at[where * half * pieces + i],
            send_sem=ssend.at[i],
            recv_sem=srecv.at[i],
            device_id=(partner, t),
            device_id_type=MESH,
        )

    odd = core == 1

    def join(i):
        k, e = half * core + i // pieces, i % pieces
        cut = slice(e * PIECE, (e + 1) * PIECE)
        to_partner(i).wait_recv()
        theirs = part_recv[i, 0:state, :].astype(jnp.float32)
        tail = part_recv[i, state : state + EXTRA, :].astype(jnp.float32)
        their_decay = tail[0:1] + tail[1:2]
        mine = states[k][:, cut]
        my_decay = decays[k][0:1, cut]
        first = jnp.where(odd, theirs, mine)
        second = jnp.where(odd, mine, theirs)
        first_decay = jnp.where(odd, their_decay, my_decay)
        second_decay = jnp.where(odd, my_decay, their_decay)
        total = second_decay * first + second

        @pl.when((pair == 0) & (pairs > 1))
        def _():
            chain_send[i] = total.astype(jnp.bfloat16)
            for r in range(parts):
                chain(i, r).start()

        pair_state[i] = total
        pair_decay[i] = jnp.broadcast_to(second_decay * first_decay, (8, PIECE))
        middle[i] = first
        first_decays[i] = jnp.broadcast_to(first_decay, (8, PIECE))

    def step(i, entry):
        place = core * half * pieces + i
        if entry:
            for r in range(parts):
                band = slice(r * ROWS, (r + 1) * ROWS)
                chain(i, r).wait_recv()
                came = chain_recv[i, band, :].astype(jnp.float32)

                @pl.when(pair < pairs - 1)
                def _():
                    leaving = pair_decay[i][0:1] * came + pair_state[i, band, :]
                    chain_send[i, band, :] = leaving.astype(jnp.bfloat16)
                    chain(i, r).start()

                between = first_decays[i][0:1] * came + middle[i, band, :]
                share_send[i, band, :] = jnp.where(odd, came, between).astype(jnp.bfloat16)
                entering[place, band, :] = jnp.where(odd, between, came).astype(jnp.bfloat16)
        else:
            came = jnp.zeros((state, PIECE), jnp.float32)
            between = middle[i]
            share_send[i] = jnp.where(odd, came, between).astype(jnp.bfloat16)
            entering[place] = jnp.where(odd, between, came).astype(jnp.bfloat16)
        share(i, core).start()

    @pl.when(pair == 0)
    def _():
        for i in range(half * pieces):
            join(i)

    cm = conv(inner + state, state).astype(jnp.bfloat16)
    cs2 = cs * LOG2E
    cs2t = cst * LOG2E
    row2 = jnp.where(dt > 0.0, cs2 - jnp.log(dt) * LOG2E, 3e38)
    scores = dot(cm, bt)
    top = jnp.where(keep, scores[:q, :q], 0.0)
    side = scores[q:, :q]
    end = jnp.where(keep, scores[q:, q:], 0.0)

    def mix_of(h):
        c0, c1 = cs2t[:q, h : h + 1], cs2t[q:, h : h + 1]
        r0, r1 = row2[h : h + 1, :q], row2[h : h + 1, q:]
        m0 = jnp.where(keep, top * jnp.exp2(c0 - r0), 0.0).astype(jnp.bfloat16)
        m1 = (side * jnp.exp2(c1 - r0)).astype(jnp.bfloat16)
        m2 = jnp.where(keep, end * jnp.exp2(c1 - r1), 0.0).astype(jnp.bfloat16)
        return m0, jnp.concatenate([m1, m2], axis=1)

    def intra(k):
        for p in range(per // 2):
            pairx = xs[k, :, p * 2 * head_dim : (p + 1) * 2 * head_dim]
            got = []
            for e in range(2):
                m0, m1 = mix_of(k * per + 2 * p + e)
                got.append(jnp.concatenate([dot(m0, pairx[:q]), dot(m1, pairx)], axis=0))
            y_in[k, :, p * 2 * head_dim : (p + 1) * 2 * head_dim] = jnp.where(low, got[0], got[1])

    for k in range(chunks):
        intra(k)
        if k == 0:

            @pl.when(pair > 0)
            def _():
                for i in range(half * pieces):
                    join(i)

            @pl.when(pair == 0)
            def _():
                for i in range(half * pieces):
                    step(i, False)

        if k != 1 and k < chunks - 1:

            @pl.when(pair == max(k, 1))
            def _():
                for i in range(half * pieces):
                    step(i, True)

    grown = expand(jnp.exp(cst), slice(None))
    for k in range(chunks):
        ecs[k] = grown[:, k * CHUNK : (k + 1) * CHUNK]
    loads[8].wait()
    gated = silu(dot(nm[HALO:, :], w_gate[...]).astype(jnp.bfloat16).astype(jnp.float32))
    for k in range(chunks):
        gate[k] = gated[:, k * CHUNK : (k + 1) * CHUNK]
    loads[9].wait()
    loads[10].wait()
    out_row[...] = norm_out[...][None, :]

    def finish(k, square, total):
        entry = jnp.concatenate([entering[k * pieces + e] for e in range(pieces)], axis=1)
        start = pl.multiple_of(k * CHUNK, CHUNK)
        g = (y_in[k] + ecs[k] * dot(cm, entry)) * gate[k]
        square = square + jnp.sum(g * g, axis=-1, keepdims=True)
        scaled = (g * out_row[:, pl.ds(start, CHUNK)]).astype(jnp.bfloat16)
        return square, total + dot(scaled, w_out[pl.ds(start, CHUNK), :])

    square = jnp.zeros((length, 1), jnp.float32)
    total = jnp.zeros((length, out.shape[1]), jnp.float32)
    for j in range(half):

        @pl.when(pair >= chunks - 1)
        def _():
            for e in range(pieces):
                step(j * pieces + e, True)

        square, total = finish(half * core + j, square, total)
    for j in range(half):
        for e in range(pieces):
            share(j * pieces + e, 1 - core).wait_recv()
        square, total = finish(half * (1 - core) + j, square, total)
    out[...] = (total * lax.rsqrt(square / inner + epsilon)).astype(out.dtype)

    for peer in peers:
        for r in range(2):
            across(r, peer, t).wait_send()

    @pl.when(s < seqs - 1)
    def _():
        for h in range(tables):
            rim(s + 1, h, t).wait_send()

    for i in range(half * pieces):
        to_partner(i).wait_send()
        share(i, core).wait_send()

    @pl.when(pair < pairs - 1)
    def _():
        for i in range(half * pieces):
            for r in range(parts):
                chain(i, r).wait_send()


def move(got, out, sem):
    size = got.shape[0] // 4
    copies = [
        pltpu.make_async_copy(
            got.at[pl.ds(i * size, size)], out.at[0, pl.ds(i * size, size)], sem.at[i]
        )
        for i in range(4)
    ]
    for copy in copies:
        copy.start()
    for copy in copies:
        copy.wait()


def local(tables, seqs, *args):
    args = args[:5] + (args[5].T,) + args[6:]
    columns, gaps, norm_in, w_gate, w_xbc, w_step = args[:6]
    step_bias, conv_weight, conv_bias, rates, norm_out, w_out = args[6:]
    length = columns.shape[1]
    inner = w_gate.shape[1]
    state = (w_xbc.shape[1] - inner) // 2
    chunks = inner // CHUNK
    count = chunks // 2 * (CHUNK // PIECE)
    f32, bf16 = jnp.float32, jnp.bfloat16
    dma = pltpu.SemaphoreType.DMA
    scratch = [pltpu.VMEM(a.shape, a.dtype) for a in args[1:]]
    scratch += [
        pltpu.VMEM((tables, HALO + length, columns.shape[2]), bf16),
        pltpu.VMEM((HALO + length, w_xbc.shape[1]), f32),
        pltpu.VMEM((chunks, length, CHUNK), bf16),
        pltpu.VMEM((chunks, length, CHUNK), f32),
        pltpu.VMEM((chunks, length, CHUNK), f32),
        pltpu.VMEM((chunks, length, CHUNK), f32),
        pltpu.VMEM((chunks, state, CHUNK), f32),
        pltpu.VMEM((chunks, 8, CHUNK), f32),
        pltpu.VMEM((count, state, PIECE), f32),
        pltpu.VMEM((count, 8, PIECE), f32),
        pltpu.VMEM((count, 8, PIECE), f32),
        pltpu.VMEM((count, state, PIECE), f32),
        pltpu.VMEM((2 * count, state, PIECE), bf16),
        pltpu.VMEM((count, state + EXTRA, PIECE), bf16),
        pltpu.VMEM((count, state + EXTRA, PIECE), bf16),
        pltpu.VMEM((count, state, PIECE), bf16),
        pltpu.VMEM((count, state, PIECE), bf16),
        pltpu.VMEM((count, state, PIECE), bf16),
        pltpu.VMEM((rates.shape[0], inner), bf16),
        pltpu.VMEM((HALO + length, w_gate.shape[0]), bf16),
        pltpu.VMEM((1, w_xbc.shape[1]), f32),
        pltpu.VMEM((1, inner), f32),
        dma((11,)),
        dma(()),
        dma((2, tables)),
        dma((2, tables)),
        dma((tables,)),
        dma((tables,)),
        dma((count,)),
        dma((count,)),
        dma((count, state // ROWS)),
        dma((count, state // ROWS)),
        dma((count,)),
        dma((count,)),
    ]
    got = pl.pallas_call(
        functools.partial(kernel, tables, seqs),
        out_shape=jax.ShapeDtypeStruct((length, w_out.shape[1]), bf16),
        in_specs=[pl.BlockSpec(memory_space=pltpu.HBM)] * len(args),
        out_specs=pl.BlockSpec(memory_space=pltpu.VMEM),
        scratch_shapes=scratch,
        compiler_params=pltpu.CompilerParams(
            collective_id=0, has_side_effects=True, vmem_limit_bytes=63 * 2**20
        ),
        cost_estimate=pl.CostEstimate(
            flops=2 * 10**9, bytes_accessed=4 * 10**6, transcendentals=2 * 10**6
        ),
    )(*args)
    return pl.pallas_call(
        move,
        out_shape=jax.ShapeDtypeStruct((1,) + got.shape, got.dtype),
        in_specs=[pl.BlockSpec(memory_space=pl.ANY)],
        out_specs=pl.BlockSpec(memory_space=pl.ANY),
        scratch_shapes=[dma((4,))],
        compiler_params=pltpu.CompilerParams(vmem_limit_bytes=63 * 2**20),
    )(got)


def solution(mesh):
    in_specs = (P(None, "seq", "table"), P("table", "seq")) + (P(),) * 10
    return jax.shard_map(
        functools.partial(local, mesh.shape["table"], mesh.shape["seq"]),
        mesh=mesh,
        in_specs=in_specs,
        out_specs=P("table", "seq", None),
        check_vma=False,
    )
```

```python
import functools

import jax
import jax.numpy as jnp
from jax import lax
from jax.experimental import pallas as pl
from jax.experimental.pallas import tpu as pltpu
from jax.sharding import PartitionSpec as P

MESH = pl.DeviceIdType.MESH
epsilon = 1e-05
LOG2E = 1.4426950408889634
HALO = 16
CHUNK = 256
PIECE = 128
ROWS = 64
EXTRA = 16


def silu(v):
    half = 0.5 * v
    return half + half * jnp.tanh(half)


def split(v):
    hi = v.astype(jnp.bfloat16)
    return hi, (v - hi.astype(jnp.float32)).astype(jnp.bfloat16)


def dot(a, b):
    return jnp.dot(a, b, preferred_element_type=jnp.float32)


def kernel(
    tables,
    seqs,
    columns,
    gaps_h,
    norm_in_h,
    w_gate_h,
    w_xbc_h,
    w_step_h,
    step_bias_h,
    conv_weight_h,
    conv_bias_h,
    rates_h,
    norm_out_h,
    w_out_h,
    out,
    gaps,
    norm_in,
    w_gate,
    w_xbc,
    w_step,
    step_bias,
    conv_weight,
    conv_bias,
    rates,
    norm_out,
    w_out,
    cols,
    xb,
    xs,
    y_in,
    ecs,
    gate,
    states,
    decays,
    pair_state,
    pair_decay,
    first_decays,
    middle,
    entering,
    part_send,
    part_recv,
    chain_send,
    chain_recv,
    share_send,
    spread_s,
    nm,
    mids,
    bias_row,
    out_row,
    load_sem,
    own_sem,
    all_send,
    all_recv,
    halo_send,
    halo_recv,
    psend,
    precv,
    csend,
    crecv,
    ssend,
    srecv,
):
    s = lax.axis_index("seq")
    t = lax.axis_index("table")
    core = lax.rem(s, 2)
    pair = s // 2
    pairs = seqs // 2
    partner = s + 1 - 2 * core
    length = gaps.shape[1]
    inner = w_gate.shape[1]
    heads = rates.shape[0]
    pieces = CHUNK // PIECE
    head_dim = inner // heads
    state = (w_xbc.shape[1] - inner) // 2
    parts = state // ROWS
    taps = conv_weight.shape[0]
    chunks = inner // CHUNK
    half = chunks // 2
    per = CHUNK // head_dim

    sources = (w_xbc_h, w_step_h, norm_in_h, conv_weight_h, conv_bias_h, gaps_h)
    sources += (rates_h, step_bias_h, w_gate_h, norm_out_h, w_out_h)
    places = (w_xbc, w_step, norm_in, conv_weight, conv_bias, gaps)
    places += (rates, step_bias, w_gate, norm_out, w_out)
    loads = [
        pltpu.make_async_copy(a, b, load_sem.at[i])
        for i, (a, b) in enumerate(zip(sources, places))
    ]
    own = pltpu.make_async_copy(columns.at[t], cols.at[t, pl.ds(HALO, length)], own_sem)

    barrier = pltpu.get_barrier_semaphore()

    def greet(where):
        pl.semaphore_signal(barrier, inc=1, device_id=where, device_id_type=MESH)

    for off in range(1, tables):
        greet((s, lax.rem(t + off, tables)))
    greet((partner, t))

    @pl.when(s > 0)
    def _():
        for h in range(tables):
            greet((s - 1, h))

    @pl.when(s < seqs - 1)
    def _():
        for h in range(tables):
            greet((s + 1, h))

    @pl.when(pair > 0)
    def _():
        greet((s - 2, t))

    @pl.when(pair < pairs - 1)
    def _():
        greet((s + 2, t))

    own.start()
    for load in loads:
        load.start()

    @pl.when(s == 0)
    def _():
        for h in range(tables):
            cols[h, 0:HALO, :] = jnp.zeros((HALO, cols.shape[2]), cols.dtype)

    def count(held):
        return jnp.where(held, 1, 0)

    pl.semaphore_wait(
        barrier,
        tables
        + tables * (count(s > 0) + count(s < seqs - 1))
        + count(pair > 0)
        + count(pair < pairs - 1),
    )

    q = length // 2

    def across(r, peer, sender):
        return pltpu.make_async_remote_copy(
            src_ref=columns.at[peer, pl.ds(r * q, q)],
            dst_ref=cols.at[sender, pl.ds(HALO + r * q, q)],
            send_sem=all_send.at[r, peer],
            recv_sem=all_recv.at[r, sender],
            device_id=(s, peer),
            device_id_type=MESH,
        )

    def rim(target, peer, sender):
        return pltpu.make_async_remote_copy(
            src_ref=columns.at[peer, pl.ds(length - HALO, HALO)],
            dst_ref=cols.at[sender, pl.ds(0, HALO)],
            send_sem=halo_send.at[peer],
            recv_sem=halo_recv.at[sender],
            device_id=(target, peer),
            device_id_type=MESH,
        )

    peers = [lax.rem(t + off, tables) for off in range(1, tables)]
    for peer in peers:
        across(0, peer, t).start()

    @pl.when(s < seqs - 1)
    def _():
        for h in range(tables):
            rim(s + 1, h, t).start()

    for peer in peers:
        across(1, peer, t).start()

    lane = lax.broadcasted_iota(jnp.int32, (heads, inner), 1) // head_dim
    head = lax.broadcasted_iota(jnp.int32, (heads, inner), 0)
    spread_s[...] = jnp.where(lane == head, 1.0, 0.0).astype(jnp.bfloat16)
    before = lax.broadcasted_iota(jnp.int32, (q, q), 0)
    after = lax.broadcasted_iota(jnp.int32, (q, q), 1)
    upper = jnp.where(before <= after, 1.0, 0.0).astype(jnp.bfloat16)
    keep = lax.broadcasted_iota(jnp.int32, (q, q), 0) >= lax.broadcasted_iota(
        jnp.int32, (q, q), 1
    )
    low = lax.broadcasted_iota(jnp.int32, (length, 2 * head_dim), 1) < head_dim

    def expand(v, lanes):
        hi, lo = split(v)
        return dot(hi, spread_s[:, lanes]) + dot(lo, spread_s[:, lanes])

    for load in loads[:8]:
        load.wait()
    own.wait()
    bias_row[...] = conv_bias[...][None, :]

    def norm(begin, end):
        u = jnp.concatenate([cols[h, begin:end, :] for h in range(tables)], axis=1)
        u = u.astype(jnp.float32)
        scale = lax.rsqrt(jnp.mean(u * u, axis=-1, keepdims=True) + epsilon)
        nm[begin:end, :] = (u * scale * norm_in[...][None, :]).astype(jnp.bfloat16)

    def project(begin, end, lanes):
        made = dot(nm[begin:end, :], w_xbc[:, lanes])
        xb[begin:end, lanes] = made.astype(jnp.bfloat16).astype(jnp.float32)

    for peer in peers:
        across(0, peer, peer).wait_recv()

    @pl.when(s > 0)
    def _():
        for h in range(tables):
            rim(s, h, h).wait_recv()

    def times(g):
        here = nm[HALO + g * q : HALO + (g + 1) * q, :]
        raw = lax.dot_general(
            w_step[...], here, (((1,), (1,)), ((), ())), preferred_element_type=jnp.float32
        )
        raw = raw + step_bias[...][:, None]
        dt = jnp.maximum(raw, 0.0) + jnp.log1p(jnp.exp(-jnp.abs(raw)))
        da = -rates[...][:, None] * dt * gaps[:, g * q : (g + 1) * q]
        d1 = da.astype(jnp.bfloat16)
        d2, d3 = split(da - d1.astype(jnp.float32))
        cs = dot(d1, upper) + (dot(d2, upper) + dot(d3, upper))
        faded = (jnp.exp(cs[:, q - 1 : q] - cs) * dt).T
        return dt, cs, faded

    def conv(start, width, begin, count):
        lanes = pl.ds(start, width)
        total = bias_row[:, lanes]
        for k in range(taps):
            total = total + conv_weight[pl.ds(k, 1), lanes] * xb[
                pl.ds(HALO - taps + 1 + k + begin, count), lanes
            ]
        return silu(total)

    def half_state(k, g, bt, faded):
        start = k * CHUNK if g == 0 else pl.multiple_of(k * CHUNK, CHUNK)
        x = conv(start, CHUNK, g * q, q).astype(jnp.bfloat16)
        xs[k, g * q : (g + 1) * q, :] = x
        weighted = expand(faded, pl.ds(start, CHUNK)) * x.astype(jnp.float32)
        return dot(bt, weighted.astype(jnp.bfloat16))

    norm(0, HALO + q)
    project(0, HALO + q, slice(None))
    dt0, cs0, faded0 = times(0)
    bt0 = conv(inner, state, 0, q).T.astype(jnp.bfloat16)
    for k in range(chunks):
        states[k] = half_state(k, 0, bt0, faded0)

    for peer in peers:
        across(1, peer, peer).wait_recv()
    norm(HALO + q, HALO + length)
    dt1, cs1, faded1 = times(1)
    project(HALO + q, HALO + length, slice(inner, inner + 2 * state))
    bt1 = conv(inner, state, q, q).T.astype(jnp.bfloat16)
    closed = cs0[:, q - 1 : q]
    cs = jnp.concatenate([cs0, cs1 + closed], axis=1)
    cst = cs.T
    later = expand(jnp.exp(cs1.T[q - 16 :]), slice(None))[15:16]
    ended = expand(jnp.exp(cst[length - 16 :]), slice(None))[15:16]
    for k in range(chunks):
        cut = slice(k * CHUNK, (k + 1) * CHUNK)
        mids[k] = jnp.broadcast_to(later[:, cut], (8, CHUNK))
        decays[k] = jnp.broadcast_to(ended[:, cut], (8, CHUNK))

    def to_partner(i):
        return pltpu.make_async_remote_copy(
            src_ref=part_send.at[i],
            dst_ref=part_recv.at[i],
            send_sem=psend.at[i],
            recv_sem=precv.at[i],
            device_id=(partner, t),
            device_id_type=MESH,
        )

    rows = lax.broadcasted_iota(jnp.int32, (EXTRA, PIECE), 0)

    def chain(i, r):
        return pltpu.make_async_remote_copy(
            src_ref=chain_send.at[i, pl.ds(r * ROWS, ROWS)],
            dst_ref=chain_recv.at[i, pl.ds(r * ROWS, ROWS)],
            send_sem=csend.at[i, r],
            recv_sem=crecv.at[i, r],
            device_id=(s + 2, t),
            device_id_type=MESH,
        )

    def share(i, where):
        return pltpu.make_async_remote_copy(
            src_ref=share_send.at[i],
            dst_ref=entering.at[where * half * pieces + i],
            send_sem=ssend.at[i],
            recv_sem=srecv.at[i],
            device_id=(partner, t),
            device_id_type=MESH,
        )

    odd = core == 1

    def join(i):
        k, e = half * core + i // pieces, i % pieces
        cut = slice(e * PIECE, (e + 1) * PIECE)
        to_partner(i).wait_recv()
        theirs = part_recv[i, 0:state, :].astype(jnp.float32)
        tail = part_recv[i, state : state + EXTRA, :].astype(jnp.float32)
        their_decay = tail[0:1] + tail[1:2]
        mine = states[k][:, cut]
        my_decay = decays[k][0:1, cut]
        first = jnp.where(odd, theirs, mine)
        second = jnp.where(odd, mine, theirs)
        first_decay = jnp.where(odd, their_decay, my_decay)
        second_decay = jnp.where(odd, my_decay, their_decay)
        total = second_decay * first + second

        @pl.when((pair == 0) & (pairs > 1))
        def _():
            chain_send[i] = total.astype(jnp.bfloat16)
            for r in range(parts):
                chain(i, r).start()

        pair_state[i] = total
        pair_decay[i] = jnp.broadcast_to(second_decay * first_decay, (8, PIECE))
        middle[i] = first
        first_decays[i] = jnp.broadcast_to(first_decay, (8, PIECE))

    def step(i, entry):
        place = core * half * pieces + i
        if entry:
            for r in range(parts):
                band = slice(r * ROWS, (r + 1) * ROWS)
                chain(i, r).wait_recv()
                came = chain_recv[i, band, :].astype(jnp.float32)

                @pl.when(pair < pairs - 1)
                def _():
                    leaving = pair_decay[i][0:1] * came + pair_state[i, band, :]
                    chain_send[i, band, :] = leaving.astype(jnp.bfloat16)
                    chain(i, r).start()

                between = first_decays[i][0:1] * came + middle[i, band, :]
                share_send[i, band, :] = jnp.where(odd, came, between).astype(jnp.bfloat16)
                entering[place, band, :] = jnp.where(odd, between, came).astype(jnp.bfloat16)
        else:
            came = jnp.zeros((state, PIECE), jnp.float32)
            between = middle[i]
            share_send[i] = jnp.where(odd, came, between).astype(jnp.bfloat16)
            entering[place] = jnp.where(odd, between, came).astype(jnp.bfloat16)
        share(i, core).start()

    def first_join(j):
        @pl.when(pair == 0)
        def _():
            for e in range(pieces):
                join(j * pieces + e)

    for j in range(half):
        for mine in range(2):
            k = half * (core if mine else 1 - core) + j
            project(HALO + q, HALO + length, pl.ds(pl.multiple_of(k * CHUNK, CHUNK), CHUNK))
            made = mids[k][0:1] * states[k] + half_state(k, 1, bt1, faded1)
            if mine:
                states[k] = made
                continue
            hi, lo = split(decays[k][0:1])
            hi, lo = hi.astype(jnp.float32), lo.astype(jnp.float32)
            for e in range(pieces):
                cut = slice(e * PIECE, (e + 1) * PIECE)
                tail = jnp.where(rows == 0, hi[:, cut], jnp.where(rows == 1, lo[:, cut], 0.0))
                part_send[j * pieces + e, 0:state, :] = made[:, cut].astype(jnp.bfloat16)
                part_send[j * pieces + e, state : state + EXTRA, :] = tail.astype(jnp.bfloat16)
                to_partner(j * pieces + e).start()
            if j > 0:
                first_join(j - 1)
    first_join(half - 1)

    cm = conv(inner + state, state, 0, length).astype(jnp.bfloat16)
    bt = jnp.concatenate([bt0, bt1], axis=1)
    dt = jnp.concatenate([dt0, dt1], axis=1)
    cs2 = cs * LOG2E
    cs2t = cst * LOG2E
    row2 = jnp.where(dt > 0.0, cs2 - jnp.log(dt) * LOG2E, 3e38)
    scores = dot(cm, bt)
    top = jnp.where(keep, scores[:q, :q], 0.0)
    side = scores[q:, :q]
    end = jnp.where(keep, scores[q:, q:], 0.0)

    def mix_of(h):
        c0, c1 = cs2t[:q, h : h + 1], cs2t[q:, h : h + 1]
        r0, r1 = row2[h : h + 1, :q], row2[h : h + 1, q:]
        m0 = jnp.where(keep, top * jnp.exp2(c0 - r0), 0.0).astype(jnp.bfloat16)
        m1 = (side * jnp.exp2(c1 - r0)).astype(jnp.bfloat16)
        m2 = jnp.where(keep, end * jnp.exp2(c1 - r1), 0.0).astype(jnp.bfloat16)
        return m0, jnp.concatenate([m1, m2], axis=1)

    def intra(k):
        for p in range(per // 2):
            pairx = xs[k, :, p * 2 * head_dim : (p + 1) * 2 * head_dim]
            got = []
            for e in range(2):
                m0, m1 = mix_of(k * per + 2 * p + e)
                got.append(jnp.concatenate([dot(m0, pairx[:q]), dot(m1, pairx)], axis=0))
            y_in[k, :, p * 2 * head_dim : (p + 1) * 2 * head_dim] = jnp.where(low, got[0], got[1])

    for k in range(chunks):
        intra(k)
        if k == 0:

            @pl.when(pair > 0)
            def _():
                for i in range(half * pieces):
                    join(i)

            @pl.when(pair == 0)
            def _():
                for i in range(half * pieces):
                    step(i, False)

        if k != 1 and k < chunks - 1:

            @pl.when(pair == max(k, 1))
            def _():
                for i in range(half * pieces):
                    step(i, True)

    grown = expand(jnp.exp(cst), slice(None))
    for k in range(chunks):
        ecs[k] = grown[:, k * CHUNK : (k + 1) * CHUNK]
    loads[8].wait()
    gated = silu(dot(nm[HALO:, :], w_gate[...]).astype(jnp.bfloat16).astype(jnp.float32))
    for k in range(chunks):
        gate[k] = gated[:, k * CHUNK : (k + 1) * CHUNK]
    loads[9].wait()
    loads[10].wait()
    out_row[...] = norm_out[...][None, :]

    def finish(k, square, total):
        entry = jnp.concatenate([entering[k * pieces + e] for e in range(pieces)], axis=1)
        start = pl.multiple_of(k * CHUNK, CHUNK)
        g = (y_in[k] + ecs[k] * dot(cm, entry)) * gate[k]
        square = square + jnp.sum(g * g, axis=-1, keepdims=True)
        scaled = (g * out_row[:, pl.ds(start, CHUNK)]).astype(jnp.bfloat16)
        return square, total + dot(scaled, w_out[pl.ds(start, CHUNK), :])

    square = jnp.zeros((length, 1), jnp.float32)
    total = jnp.zeros((length, out.shape[1]), jnp.float32)
    for j in range(half):

        @pl.when(pair >= chunks - 1)
        def _():
            for e in range(pieces):
                step(j * pieces + e, True)

        square, total = finish(half * core + j, square, total)
    for j in range(half):
        for e in range(pieces):
            share(j * pieces + e, 1 - core).wait_recv()
        square, total = finish(half * (1 - core) + j, square, total)
    out[...] = (total * lax.rsqrt(square / inner + epsilon)).astype(out.dtype)

    for peer in peers:
        for r in range(2):
            across(r, peer, t).wait_send()

    @pl.when(s < seqs - 1)
    def _():
        for h in range(tables):
            rim(s + 1, h, t).wait_send()

    for i in range(half * pieces):
        to_partner(i).wait_send()
        share(i, core).wait_send()

    @pl.when(pair < pairs - 1)
    def _():
        for i in range(half * pieces):
            for r in range(parts):
                chain(i, r).wait_send()


def local(tables, seqs, *args):
    args = args[:5] + (args[5].T,) + args[6:]
    columns, gaps, norm_in, w_gate, w_xbc, w_step = args[:6]
    step_bias, conv_weight, conv_bias, rates, norm_out, w_out = args[6:]
    length = columns.shape[1]
    inner = w_gate.shape[1]
    state = (w_xbc.shape[1] - inner) // 2
    chunks = inner // CHUNK
    count = chunks // 2 * (CHUNK // PIECE)
    f32, bf16 = jnp.float32, jnp.bfloat16
    dma = pltpu.SemaphoreType.DMA
    scratch = [pltpu.VMEM(a.shape, a.dtype) for a in args[1:]]
    scratch += [
        pltpu.VMEM((tables, HALO + length, columns.shape[2]), bf16),
        pltpu.VMEM((HALO + length, w_xbc.shape[1]), f32),
        pltpu.VMEM((chunks, length, CHUNK), bf16),
        pltpu.VMEM((chunks, length, CHUNK), f32),
        pltpu.VMEM((chunks, length, CHUNK), f32),
        pltpu.VMEM((chunks, length, CHUNK), f32),
        pltpu.VMEM((chunks, state, CHUNK), f32),
        pltpu.VMEM((chunks, 8, CHUNK), f32),
        pltpu.VMEM((count, state, PIECE), f32),
        pltpu.VMEM((count, 8, PIECE), f32),
        pltpu.VMEM((count, 8, PIECE), f32),
        pltpu.VMEM((count, state, PIECE), f32),
        pltpu.VMEM((2 * count, state, PIECE), bf16),
        pltpu.VMEM((count, state + EXTRA, PIECE), bf16),
        pltpu.VMEM((count, state + EXTRA, PIECE), bf16),
        pltpu.VMEM((count, state, PIECE), bf16),
        pltpu.VMEM((count, state, PIECE), bf16),
        pltpu.VMEM((count, state, PIECE), bf16),
        pltpu.VMEM((rates.shape[0], inner), bf16),
        pltpu.VMEM((HALO + length, w_gate.shape[0]), bf16),
        pltpu.VMEM((chunks, 8, CHUNK), f32),
        pltpu.VMEM((1, w_xbc.shape[1]), f32),
        pltpu.VMEM((1, inner), f32),
        dma((11,)),
        dma(()),
        dma((2, tables)),
        dma((2, tables)),
        dma((tables,)),
        dma((tables,)),
        dma((count,)),
        dma((count,)),
        dma((count, state // ROWS)),
        dma((count, state // ROWS)),
        dma((count,)),
        dma((count,)),
    ]
    got = pl.pallas_call(
        functools.partial(kernel, tables, seqs),
        out_shape=pltpu.VMEM((length, w_out.shape[1]), bf16),
        in_specs=[pl.BlockSpec(memory_space=pltpu.HBM)] * len(args),
        out_specs=pl.BlockSpec(memory_space=pltpu.VMEM),
        scratch_shapes=scratch,
        compiler_params=pltpu.CompilerParams(
            collective_id=0, has_side_effects=True, vmem_limit_bytes=60 * 10**6
        ),
        cost_estimate=pl.CostEstimate(
            flops=2 * 10**9, bytes_accessed=4 * 10**6, transcendentals=2 * 10**6
        ),
    )(*args)
    return got[None]


def solution(mesh):
    in_specs = (P(None, "seq", "table"), P("table", "seq")) + (P(),) * 10
    return jax.shard_map(
        functools.partial(local, mesh.shape["table"], mesh.shape["seq"]),
        mesh=mesh,
        in_specs=in_specs,
        out_specs=P("table", "seq", None),
        check_vma=False,
    )
```

```python
import functools

import jax
import jax.numpy as jnp
from jax import lax
from jax.experimental import pallas as pl
from jax.experimental.pallas import tpu as pltpu
from jax.sharding import PartitionSpec as P

MESH = pl.DeviceIdType.MESH
epsilon = 1e-05
LOG2E = 1.4426950408889634
HALO = 16
CHUNK = 256
PIECE = 128
ROWS = 64
EXTRA = 16


def silu(v):
    half = 0.5 * v
    return half + half * jnp.tanh(half)


def split(v):
    hi = v.astype(jnp.bfloat16)
    return hi, (v - hi.astype(jnp.float32)).astype(jnp.bfloat16)


def dot(a, b):
    return jnp.dot(a, b, preferred_element_type=jnp.float32)


def kernel(
    tables,
    seqs,
    columns,
    gaps_h,
    norm_in_h,
    w_gate_h,
    w_xbc_h,
    w_step_h,
    step_bias_h,
    conv_weight_h,
    conv_bias_h,
    rates_h,
    norm_out_h,
    w_out_h,
    out,
    gaps,
    norm_in,
    w_gate,
    w_xbc,
    w_step,
    step_bias,
    conv_weight,
    conv_bias,
    rates,
    norm_out,
    w_out,
    cols,
    xb,
    xs,
    y_in,
    ecs,
    gate,
    states,
    decays,
    pair_state,
    pair_decay,
    first_decays,
    middle,
    entering,
    part_send,
    part_recv,
    chain_send,
    chain_recv,
    share_send,
    spread_s,
    nm,
    mids,
    bias_row,
    out_row,
    load_sem,
    own_sem,
    all_send,
    all_recv,
    halo_send,
    halo_recv,
    psend,
    precv,
    csend,
    crecv,
    ssend,
    srecv,
):
    s = lax.axis_index("seq")
    t = lax.axis_index("table")
    core = lax.rem(s, 2)
    pair = s // 2
    pairs = seqs // 2
    partner = s + 1 - 2 * core
    length = gaps.shape[1]
    inner = w_gate.shape[1]
    heads = rates.shape[0]
    pieces = CHUNK // PIECE
    head_dim = inner // heads
    state = (w_xbc.shape[1] - inner) // 2
    parts = state // ROWS
    taps = conv_weight.shape[0]
    chunks = inner // CHUNK
    half = chunks // 2
    per = CHUNK // head_dim

    sources = (w_xbc_h, w_step_h, norm_in_h, conv_weight_h, conv_bias_h, gaps_h)
    sources += (rates_h, step_bias_h, w_gate_h, norm_out_h, w_out_h)
    places = (w_xbc, w_step, norm_in, conv_weight, conv_bias, gaps)
    places += (rates, step_bias, w_gate, norm_out, w_out)
    loads = [
        pltpu.make_async_copy(a, b, load_sem.at[i])
        for i, (a, b) in enumerate(zip(sources, places))
    ]
    own = pltpu.make_async_copy(columns.at[t], cols.at[t, pl.ds(HALO, length)], own_sem)

    barrier = pltpu.get_barrier_semaphore()

    def greet(where):
        pl.semaphore_signal(barrier, inc=1, device_id=where, device_id_type=MESH)

    for off in range(1, tables):
        greet((s, lax.rem(t + off, tables)))
    for h in range(tables):
        greet((partner, h))

    own.start()
    for load in loads:
        load.start()

    @pl.when(s == 0)
    def _():
        for h in range(tables):
            cols[h, 0:HALO, :] = jnp.zeros((HALO, cols.shape[2]), cols.dtype)

    def count(held):
        return jnp.where(held, 1, 0)

    earlier = count(pair > 0)
    pl.semaphore_wait(
        barrier, 2 * tables - 1 + earlier * (1 + tables * (1 - core))
    )

    q = length // 2

    def across(r, peer, sender):
        return pltpu.make_async_remote_copy(
            src_ref=columns.at[peer, pl.ds(r * q, q)],
            dst_ref=cols.at[sender, pl.ds(HALO + r * q, q)],
            send_sem=all_send.at[r, peer],
            recv_sem=all_recv.at[r, sender],
            device_id=(s, peer),
            device_id_type=MESH,
        )

    def rim(target, peer, sender):
        return pltpu.make_async_remote_copy(
            src_ref=columns.at[peer, pl.ds(length - HALO, HALO)],
            dst_ref=cols.at[sender, pl.ds(0, HALO)],
            send_sem=halo_send.at[peer],
            recv_sem=halo_recv.at[sender],
            device_id=(target, peer),
            device_id_type=MESH,
        )

    peers = [lax.rem(t + off, tables) for off in range(1, tables)]
    for peer in peers:
        across(0, peer, t).start()

    @pl.when(core == 0)
    def _():
        for h in range(tables):
            rim(s + 1, h, t).start()

    for peer in peers:
        across(1, peer, t).start()

    @pl.when(pair < pairs - 1)
    def _():
        greet((s + 2, t))

    @pl.when((pair < pairs - 1) & (core == 1))
    def _():
        for h in range(tables):
            greet((s + 1, h))

    @pl.when(pair > 0)
    def _():
        greet((s - 2, t))

    @pl.when((pair > 0) & (core == 0))
    def _():
        for h in range(tables):
            greet((s - 1, h))

    lane = lax.broadcasted_iota(jnp.int32, (heads, inner), 1) // head_dim
    head = lax.broadcasted_iota(jnp.int32, (heads, inner), 0)
    spread_s[...] = jnp.where(lane == head, 1.0, 0.0).astype(jnp.bfloat16)
    before = lax.broadcasted_iota(jnp.int32, (q, q), 0)
    after = lax.broadcasted_iota(jnp.int32, (q, q), 1)
    upper = jnp.where(before <= after, 1.0, 0.0).astype(jnp.bfloat16)
    keep = lax.broadcasted_iota(jnp.int32, (q, q), 0) >= lax.broadcasted_iota(
        jnp.int32, (q, q), 1
    )
    low = lax.broadcasted_iota(jnp.int32, (length, 2 * head_dim), 1) < head_dim

    def expand(v, lanes):
        hi, lo = split(v)
        return dot(hi, spread_s[:, lanes]) + dot(lo, spread_s[:, lanes])

    @pl.when(pair < pairs - 1)
    def _():
        pl.semaphore_wait(barrier, 1 + tables * core)

    @pl.when((pair < pairs - 1) & (core == 1))
    def _():
        for h in range(tables):
            rim(s + 1, h, t).start()

    for load in loads[:8]:
        load.wait()
    own.wait()
    bias_row[...] = conv_bias[...][None, :]

    def norm(begin, end):
        u = jnp.concatenate([cols[h, begin:end, :] for h in range(tables)], axis=1)
        u = u.astype(jnp.float32)
        scale = lax.rsqrt(jnp.mean(u * u, axis=-1, keepdims=True) + epsilon)
        nm[begin:end, :] = (u * scale * norm_in[...][None, :]).astype(jnp.bfloat16)

    def project(begin, end, lanes):
        made = dot(nm[begin:end, :], w_xbc[:, lanes])
        xb[begin:end, lanes] = made.astype(jnp.bfloat16).astype(jnp.float32)

    for peer in peers:
        across(0, peer, peer).wait_recv()

    @pl.when(s > 0)
    def _():
        for h in range(tables):
            rim(s, h, h).wait_recv()

    def times(g):
        here = nm[HALO + g * q : HALO + (g + 1) * q, :]
        raw = lax.dot_general(
            w_step[...], here, (((1,), (1,)), ((), ())), preferred_element_type=jnp.float32
        )
        raw = raw + step_bias[...][:, None]
        dt = jnp.maximum(raw, 0.0) + jnp.log1p(jnp.exp(-jnp.abs(raw)))
        da = -rates[...][:, None] * dt * gaps[:, g * q : (g + 1) * q]
        d1 = da.astype(jnp.bfloat16)
        d2, d3 = split(da - d1.astype(jnp.float32))
        cs = dot(d1, upper) + (dot(d2, upper) + dot(d3, upper))
        faded = (jnp.exp(cs[:, q - 1 : q] - cs) * dt).T
        return dt, cs, faded

    def conv(start, width, begin, count):
        lanes = pl.ds(start, width)
        total = bias_row[:, lanes]
        for k in range(taps):
            total = total + conv_weight[pl.ds(k, 1), lanes] * xb[
                pl.ds(HALO - taps + 1 + k + begin, count), lanes
            ]
        return silu(total)

    def half_state(k, g, bt, faded):
        start = k * CHUNK if g == 0 else pl.multiple_of(k * CHUNK, CHUNK)
        x = conv(start, CHUNK, g * q, q).astype(jnp.bfloat16)
        xs[k, g * q : (g + 1) * q, :] = x
        weighted = expand(faded, pl.ds(start, CHUNK)) * x.astype(jnp.float32)
        return dot(bt, weighted.astype(jnp.bfloat16))

    norm(0, HALO + q)
    project(0, HALO + q, slice(None))
    dt0, cs0, faded0 = times(0)
    bt0 = conv(inner, state, 0, q).T.astype(jnp.bfloat16)
    for k in range(chunks):
        states[k] = half_state(k, 0, bt0, faded0)

    for peer in peers:
        across(1, peer, peer).wait_recv()
    norm(HALO + q, HALO + length)
    dt1, cs1, faded1 = times(1)
    project(HALO + q, HALO + length, slice(inner, inner + 2 * state))
    bt1 = conv(inner, state, q, q).T.astype(jnp.bfloat16)
    closed = cs0[:, q - 1 : q]
    cs = jnp.concatenate([cs0, cs1 + closed], axis=1)
    cst = cs.T
    later = expand(jnp.exp(cs1.T[q - 16 :]), slice(None))[15:16]
    ended = expand(jnp.exp(cst[length - 16 :]), slice(None))[15:16]
    for k in range(chunks):
        cut = slice(k * CHUNK, (k + 1) * CHUNK)
        mids[k] = jnp.broadcast_to(later[:, cut], (8, CHUNK))
        decays[k] = jnp.broadcast_to(ended[:, cut], (8, CHUNK))

    def to_partner(i):
        return pltpu.make_async_remote_copy(
            src_ref=part_send.at[i],
            dst_ref=part_recv.at[i],
            send_sem=psend.at[i],
            recv_sem=precv.at[i],
            device_id=(partner, t),
            device_id_type=MESH,
        )

    rows = lax.broadcasted_iota(jnp.int32, (EXTRA, PIECE), 0)

    def chain(i, r):
        return pltpu.make_async_remote_copy(
            src_ref=chain_send.at[i, pl.ds(r * ROWS, ROWS)],
            dst_ref=chain_recv.at[i, pl.ds(r * ROWS, ROWS)],
            send_sem=csend.at[i, r],
            recv_sem=crecv.at[i, r],
            device_id=(s + 2, t),
            device_id_type=MESH,
        )

    def share(i, where):
        return pltpu.make_async_remote_copy(
            src_ref=share_send.at[i],
            dst_ref=entering.at[where * half * pieces + i],
            send_sem=ssend.at[i],
            recv_sem=srecv.at[i],
            device_id=(partner, t),
            device_id_type=MESH,
        )

    odd = core == 1

    def join(i):
        k, e = half * core + i // pieces, i % pieces
        cut = slice(e * PIECE, (e + 1) * PIECE)
        to_partner(i).wait_recv()
        theirs = part_recv[i, 0:state, :].astype(jnp.float32)
        tail = part_recv[i, state : state + EXTRA, :].astype(jnp.float32)
        their_decay = tail[0:1] + tail[1:2]
        mine = states[k][:, cut]
        my_decay = decays[k][0:1, cut]
        first = jnp.where(odd, theirs, mine)
        second = jnp.where(odd, mine, theirs)
        first_decay = jnp.where(odd, their_decay, my_decay)
        second_decay = jnp.where(odd, my_decay, their_decay)
        total = second_decay * first + second

        @pl.when((pair == 0) & (pairs > 1))
        def _():
            chain_send[i] = total.astype(jnp.bfloat16)
            for r in range(parts):
                chain(i, r).start()

        pair_state[i] = total
        pair_decay[i] = jnp.broadcast_to(second_decay * first_decay, (8, PIECE))
        middle[i] = first
        first_decays[i] = jnp.broadcast_to(first_decay, (8, PIECE))

    def step(i, entry):
        place = core * half * pieces + i
        if entry:
            for r in range(parts):
                band = slice(r * ROWS, (r + 1) * ROWS)
                chain(i, r).wait_recv()
                came = chain_recv[i, band, :].astype(jnp.float32)

                @pl.when(pair < pairs - 1)
                def _():
                    leaving = pair_decay[i][0:1] * came + pair_state[i, band, :]
                    chain_send[i, band, :] = leaving.astype(jnp.bfloat16)
                    chain(i, r).start()

                between = first_decays[i][0:1] * came + middle[i, band, :]
                share_send[i, band, :] = jnp.where(odd, came, between).astype(jnp.bfloat16)
                entering[place, band, :] = jnp.where(odd, between, came).astype(jnp.bfloat16)
        else:
            came = jnp.zeros((state, PIECE), jnp.float32)
            between = middle[i]
            share_send[i] = jnp.where(odd, came, between).astype(jnp.bfloat16)
            entering[place] = jnp.where(odd, between, came).astype(jnp.bfloat16)
        share(i, core).start()

    def first_join(j):
        @pl.when(pair == 0)
        def _():
            for e in range(pieces):
                join(j * pieces + e)

    for j in range(half):
        for mine in range(2):
            k = half * (core if mine else 1 - core) + j
            project(HALO + q, HALO + length, pl.ds(pl.multiple_of(k * CHUNK, CHUNK), CHUNK))
            made = mids[k][0:1] * states[k] + half_state(k, 1, bt1, faded1)
            if mine:
                states[k] = made
                continue
            hi, lo = split(decays[k][0:1])
            hi, lo = hi.astype(jnp.float32), lo.astype(jnp.float32)
            for e in range(pieces):
                cut = slice(e * PIECE, (e + 1) * PIECE)
                tail = jnp.where(rows == 0, hi[:, cut], jnp.where(rows == 1, lo[:, cut], 0.0))
                part_send[j * pieces + e, 0:state, :] = made[:, cut].astype(jnp.bfloat16)
                part_send[j * pieces + e, state : state + EXTRA, :] = tail.astype(jnp.bfloat16)
                to_partner(j * pieces + e).start()
            if j > 0:
                first_join(j - 1)
    first_join(half - 1)

    cm = conv(inner + state, state, 0, length).astype(jnp.bfloat16)
    bt = jnp.concatenate([bt0, bt1], axis=1)
    dt = jnp.concatenate([dt0, dt1], axis=1)
    cs2 = cs * LOG2E
    cs2t = cst * LOG2E
    row2 = jnp.where(dt > 0.0, cs2 - jnp.log(dt) * LOG2E, 3e38)
    scores = dot(cm, bt)
    top = jnp.where(keep, scores[:q, :q], 0.0)
    side = scores[q:, :q]
    end = jnp.where(keep, scores[q:, q:], 0.0)

    def mix_of(h):
        c0, c1 = cs2t[:q, h : h + 1], cs2t[q:, h : h + 1]
        r0, r1 = row2[h : h + 1, :q], row2[h : h + 1, q:]
        m0 = jnp.where(keep, top * jnp.exp2(c0 - r0), 0.0).astype(jnp.bfloat16)
        m1 = (side * jnp.exp2(c1 - r0)).astype(jnp.bfloat16)
        m2 = jnp.where(keep, end * jnp.exp2(c1 - r1), 0.0).astype(jnp.bfloat16)
        return m0, jnp.concatenate([m1, m2], axis=1)

    def intra(k):
        for p in range(per // 2):
            pairx = xs[k, :, p * 2 * head_dim : (p + 1) * 2 * head_dim]
            got = []
            for e in range(2):
                m0, m1 = mix_of(k * per + 2 * p + e)
                got.append(jnp.concatenate([dot(m0, pairx[:q]), dot(m1, pairx)], axis=0))
            y_in[k, :, p * 2 * head_dim : (p + 1) * 2 * head_dim] = jnp.where(low, got[0], got[1])

    for k in range(chunks):
        intra(k)
        if k == 0:

            @pl.when(pair > 0)
            def _():
                for i in range(half * pieces):
                    join(i)

            @pl.when(pair == 0)
            def _():
                for i in range(half * pieces):
                    step(i, False)

        if k != 1 and k < chunks - 1:

            @pl.when(pair == max(k, 1))
            def _():
                for i in range(half * pieces):
                    step(i, True)

    grown = expand(jnp.exp(cst), slice(None))
    for k in range(chunks):
        ecs[k] = grown[:, k * CHUNK : (k + 1) * CHUNK]
    loads[8].wait()
    gated = silu(dot(nm[HALO:, :], w_gate[...]).astype(jnp.bfloat16).astype(jnp.float32))
    for k in range(chunks):
        gate[k] = gated[:, k * CHUNK : (k + 1) * CHUNK]
    loads[9].wait()
    loads[10].wait()
    out_row[...] = norm_out[...][None, :]

    def finish(k, square, total):
        entry = jnp.concatenate([entering[k * pieces + e] for e in range(pieces)], axis=1)
        start = pl.multiple_of(k * CHUNK, CHUNK)
        g = (y_in[k] + ecs[k] * dot(cm, entry)) * gate[k]
        square = square + jnp.sum(g * g, axis=-1, keepdims=True)
        scaled = (g * out_row[:, pl.ds(start, CHUNK)]).astype(jnp.bfloat16)
        return square, total + dot(scaled, w_out[pl.ds(start, CHUNK), :])

    square = jnp.zeros((length, 1), jnp.float32)
    total = jnp.zeros((length, out.shape[1]), jnp.float32)
    for j in range(half):

        @pl.when(pair >= chunks - 1)
        def _():
            for e in range(pieces):
                step(j * pieces + e, True)

        square, total = finish(half * core + j, square, total)
    for j in range(half):
        for e in range(pieces):
            share(j * pieces + e, 1 - core).wait_recv()
        square, total = finish(half * (1 - core) + j, square, total)
    out[...] = (total * lax.rsqrt(square / inner + epsilon)).astype(out.dtype)

    for peer in peers:
        for r in range(2):
            across(r, peer, t).wait_send()

    @pl.when(s < seqs - 1)
    def _():
        for h in range(tables):
            rim(s + 1, h, t).wait_send()

    for i in range(half * pieces):
        to_partner(i).wait_send()
        share(i, core).wait_send()

    @pl.when(pair < pairs - 1)
    def _():
        for i in range(half * pieces):
            for r in range(parts):
                chain(i, r).wait_send()


def local(tables, seqs, *args):
    args = args[:5] + (args[5].T,) + args[6:]
    columns, gaps, norm_in, w_gate, w_xbc, w_step = args[:6]
    step_bias, conv_weight, conv_bias, rates, norm_out, w_out = args[6:]
    length = columns.shape[1]
    inner = w_gate.shape[1]
    state = (w_xbc.shape[1] - inner) // 2
    chunks = inner // CHUNK
    count = chunks // 2 * (CHUNK // PIECE)
    f32, bf16 = jnp.float32, jnp.bfloat16
    dma = pltpu.SemaphoreType.DMA
    scratch = [pltpu.VMEM(a.shape, a.dtype) for a in args[1:]]
    scratch += [
        pltpu.VMEM((tables, HALO + length, columns.shape[2]), bf16),
        pltpu.VMEM((HALO + length, w_xbc.shape[1]), f32),
        pltpu.VMEM((chunks, length, CHUNK), bf16),
        pltpu.VMEM((chunks, length, CHUNK), f32),
        pltpu.VMEM((chunks, length, CHUNK), f32),
        pltpu.VMEM((chunks, length, CHUNK), f32),
        pltpu.VMEM((chunks, state, CHUNK), f32),
        pltpu.VMEM((chunks, 8, CHUNK), f32),
        pltpu.VMEM((count, state, PIECE), f32),
        pltpu.VMEM((count, 8, PIECE), f32),
        pltpu.VMEM((count, 8, PIECE), f32),
        pltpu.VMEM((count, state, PIECE), f32),
        pltpu.VMEM((2 * count, state, PIECE), bf16),
        pltpu.VMEM((count, state + EXTRA, PIECE), bf16),
        pltpu.VMEM((count, state + EXTRA, PIECE), bf16),
        pltpu.VMEM((count, state, PIECE), bf16),
        pltpu.VMEM((count, state, PIECE), bf16),
        pltpu.VMEM((count, state, PIECE), bf16),
        pltpu.VMEM((rates.shape[0], inner), bf16),
        pltpu.VMEM((HALO + length, w_gate.shape[0]), bf16),
        pltpu.VMEM((chunks, 8, CHUNK), f32),
        pltpu.VMEM((1, w_xbc.shape[1]), f32),
        pltpu.VMEM((1, inner), f32),
        dma((11,)),
        dma(()),
        dma((2, tables)),
        dma((2, tables)),
        dma((tables,)),
        dma((tables,)),
        dma((count,)),
        dma((count,)),
        dma((count, state // ROWS)),
        dma((count, state // ROWS)),
        dma((count,)),
        dma((count,)),
    ]
    got = pl.pallas_call(
        functools.partial(kernel, tables, seqs),
        out_shape=pltpu.VMEM((length, w_out.shape[1]), bf16),
        in_specs=[pl.BlockSpec(memory_space=pltpu.HBM)] * len(args),
        out_specs=pl.BlockSpec(memory_space=pltpu.VMEM),
        scratch_shapes=scratch,
        compiler_params=pltpu.CompilerParams(
            collective_id=0, has_side_effects=True, vmem_limit_bytes=60 * 10**6
        ),
        cost_estimate=pl.CostEstimate(
            flops=2 * 10**9, bytes_accessed=4 * 10**6, transcendentals=2 * 10**6
        ),
    )(*args)
    return got[None]


def solution(mesh):
    in_specs = (P(None, "seq", "table"), P("table", "seq")) + (P(),) * 10
    return jax.shard_map(
        functools.partial(local, mesh.shape["table"], mesh.shape["seq"]),
        mesh=mesh,
        in_specs=in_specs,
        out_specs=P("table", "seq", None),
        check_vma=False,
    )
```

```python
import functools

import jax
import jax.numpy as jnp
from jax import lax
from jax.experimental import pallas as pl
from jax.experimental.pallas import tpu as pltpu
from jax.sharding import PartitionSpec as P

MESH = pl.DeviceIdType.MESH
epsilon = 1e-05
LOG2E = 1.4426950408889634
HALO = 16
CHUNK = 256
PIECE = 128
ROWS = 64
EXTRA = 16


def silu(v):
    half = 0.5 * v
    return half + half * jnp.tanh(half)


def split(v):
    hi = v.astype(jnp.bfloat16)
    return hi, (v - hi.astype(jnp.float32)).astype(jnp.bfloat16)


def dot(a, b):
    return jnp.dot(a, b, preferred_element_type=jnp.float32)


def kernel(
    tables,
    seqs,
    columns,
    gaps_h,
    norm_in_h,
    w_gate_h,
    w_xbc_h,
    w_step_h,
    step_bias_h,
    conv_weight_h,
    conv_bias_h,
    rates_h,
    norm_out_h,
    w_out_h,
    out,
    gaps,
    norm_in,
    w_gate,
    w_xbc,
    w_step,
    step_bias,
    conv_weight,
    conv_bias,
    rates,
    norm_out,
    w_out,
    cols,
    xb,
    xs,
    y_in,
    ecs,
    gate,
    states,
    decays,
    pair_state,
    pair_decay,
    first_decays,
    middle,
    entering,
    part_send,
    part_recv,
    chain_send,
    chain_recv,
    share_send,
    spread_s,
    nm,
    mids,
    steep,
    rise,
    bias_row,
    out_row,
    load_sem,
    own_sem,
    all_send,
    all_recv,
    halo_send,
    halo_recv,
    psend,
    precv,
    csend,
    crecv,
    ssend,
    srecv,
):
    s = lax.axis_index("seq")
    t = lax.axis_index("table")
    core = lax.rem(s, 2)
    pair = s // 2
    pairs = seqs // 2
    partner = s + 1 - 2 * core
    length = gaps.shape[1]
    inner = w_gate.shape[1]
    heads = rates.shape[0]
    pieces = CHUNK // PIECE
    head_dim = inner // heads
    state = (w_xbc.shape[1] - inner) // 2
    parts = state // ROWS
    taps = conv_weight.shape[0]
    chunks = inner // CHUNK
    half = chunks // 2
    per = CHUNK // head_dim

    sources = (w_xbc_h, w_step_h, norm_in_h, conv_weight_h, conv_bias_h, gaps_h)
    sources += (rates_h, step_bias_h, w_gate_h, norm_out_h, w_out_h)
    places = (w_xbc, w_step, norm_in, conv_weight, conv_bias, gaps)
    places += (rates, step_bias, w_gate, norm_out, w_out)
    loads = [
        pltpu.make_async_copy(a, b, load_sem.at[i])
        for i, (a, b) in enumerate(zip(sources, places))
    ]
    own = pltpu.make_async_copy(columns.at[t], cols.at[t, pl.ds(HALO, length)], own_sem)

    barrier = pltpu.get_barrier_semaphore()

    def greet(where):
        pl.semaphore_signal(barrier, inc=1, device_id=where, device_id_type=MESH)

    for off in range(1, tables):
        greet((s, lax.rem(t + off, tables)))
    for h in range(tables):
        greet((partner, h))

    own.start()
    for load in loads:
        load.start()

    @pl.when(s == 0)
    def _():
        for h in range(tables):
            cols[h, 0:HALO, :] = jnp.zeros((HALO, cols.shape[2]), cols.dtype)

    def count(held):
        return jnp.where(held, 1, 0)

    earlier = count(pair > 0)
    pl.semaphore_wait(
        barrier, 2 * tables - 1 + earlier * (1 + tables * (1 - core))
    )

    q = length // 2

    def across(r, peer, sender):
        return pltpu.make_async_remote_copy(
            src_ref=columns.at[peer, pl.ds(r * q, q)],
            dst_ref=cols.at[sender, pl.ds(HALO + r * q, q)],
            send_sem=all_send.at[r, peer],
            recv_sem=all_recv.at[r, sender],
            device_id=(s, peer),
            device_id_type=MESH,
        )

    def rim(target, peer, sender):
        return pltpu.make_async_remote_copy(
            src_ref=columns.at[peer, pl.ds(length - HALO, HALO)],
            dst_ref=cols.at[sender, pl.ds(0, HALO)],
            send_sem=halo_send.at[peer],
            recv_sem=halo_recv.at[sender],
            device_id=(target, peer),
            device_id_type=MESH,
        )

    peers = [lax.rem(t + off, tables) for off in range(1, tables)]
    for peer in peers:
        across(0, peer, t).start()

    @pl.when(core == 0)
    def _():
        for h in range(tables):
            rim(s + 1, h, t).start()

    for peer in peers:
        across(1, peer, t).start()

    @pl.when(pair < pairs - 1)
    def _():
        greet((s + 2, t))

    @pl.when((pair < pairs - 1) & (core == 1))
    def _():
        for h in range(tables):
            greet((s + 1, h))

    @pl.when(pair > 0)
    def _():
        greet((s - 2, t))

    @pl.when((pair > 0) & (core == 0))
    def _():
        for h in range(tables):
            greet((s - 1, h))

    lane = lax.broadcasted_iota(jnp.int32, (heads, inner), 1) // head_dim
    head = lax.broadcasted_iota(jnp.int32, (heads, inner), 0)
    spread_s[...] = jnp.where(lane == head, 1.0, 0.0).astype(jnp.bfloat16)
    before = lax.broadcasted_iota(jnp.int32, (q, q), 0)
    after = lax.broadcasted_iota(jnp.int32, (q, q), 1)
    upper = jnp.where(before <= after, 1.0, 0.0).astype(jnp.bfloat16)
    keep = lax.broadcasted_iota(jnp.int32, (q, q), 0) >= lax.broadcasted_iota(
        jnp.int32, (q, q), 1
    )
    low = lax.broadcasted_iota(jnp.int32, (length, 2 * head_dim), 1) < head_dim

    def expand(v, lanes):
        hi, lo = split(v)
        return dot(hi, spread_s[:, lanes]) + dot(lo, spread_s[:, lanes])

    @pl.when(pair < pairs - 1)
    def _():
        pl.semaphore_wait(barrier, 1 + tables * core)

    @pl.when((pair < pairs - 1) & (core == 1))
    def _():
        for h in range(tables):
            rim(s + 1, h, t).start()

    for load in loads[:8]:
        load.wait()
    own.wait()
    bias_row[...] = conv_bias[...][None, :]

    def norm(begin, end):
        u = jnp.concatenate([cols[h, begin:end, :] for h in range(tables)], axis=1)
        u = u.astype(jnp.float32)
        scale = lax.rsqrt(jnp.mean(u * u, axis=-1, keepdims=True) + epsilon)
        nm[begin:end, :] = (u * scale * norm_in[...][None, :]).astype(jnp.bfloat16)

    def project(begin, end, lanes):
        made = dot(nm[begin:end, :], w_xbc[:, lanes])
        xb[begin:end, lanes] = made.astype(jnp.bfloat16).astype(jnp.float32)

    for peer in peers:
        across(0, peer, peer).wait_recv()

    @pl.when(s > 0)
    def _():
        for h in range(tables):
            rim(s, h, h).wait_recv()

    def times(g):
        here = nm[HALO + g * q : HALO + (g + 1) * q, :]
        raw = lax.dot_general(
            w_step[...], here, (((1,), (1,)), ((), ())), preferred_element_type=jnp.float32
        )
        raw = raw + step_bias[...][:, None]
        dt = jnp.maximum(raw, 0.0) + jnp.log1p(jnp.exp(-jnp.abs(raw)))
        da = -rates[...][:, None] * dt * gaps[:, g * q : (g + 1) * q]
        d1 = da.astype(jnp.bfloat16)
        d2, d3 = split(da - d1.astype(jnp.float32))
        cs = dot(d1, upper) + (dot(d2, upper) + dot(d3, upper))
        faded = (jnp.exp(cs[:, q - 1 : q] - cs) * dt).T
        return dt, cs, faded

    def conv(start, width, begin, count):
        lanes = pl.ds(start, width)
        total = bias_row[:, lanes]
        for k in range(taps):
            total = total + conv_weight[pl.ds(k, 1), lanes] * xb[
                pl.ds(HALO - taps + 1 + k + begin, count), lanes
            ]
        return silu(total)

    def half_state(k, g, bt, faded):
        start = k * CHUNK if g == 0 else pl.multiple_of(k * CHUNK, CHUNK)
        x = conv(start, CHUNK, g * q, q).astype(jnp.bfloat16)
        xs[k, g * q : (g + 1) * q, :] = x
        weighted = expand(faded, pl.ds(start, CHUNK)) * x.astype(jnp.float32)
        return dot(bt, weighted.astype(jnp.bfloat16))

    norm(0, HALO + q)
    project(0, HALO + q, slice(None))
    dt0, cs0, faded0 = times(0)
    bt0 = conv(inner, state, 0, q).T.astype(jnp.bfloat16)
    for k in range(chunks):
        states[k] = half_state(k, 0, bt0, faded0)

    for peer in peers:
        across(1, peer, peer).wait_recv()
    norm(HALO + q, HALO + length)
    dt1, cs1, faded1 = times(1)
    project(HALO + q, HALO + length, slice(inner, inner + 2 * state))
    bt1 = conv(inner, state, q, q).T.astype(jnp.bfloat16)
    closed = cs0[:, q - 1 : q]
    cs = jnp.concatenate([cs0, cs1 + closed], axis=1)
    cst = cs.T
    later = expand(jnp.exp(cs1.T[q - 16 :]), slice(None))[15:16]
    ended = expand(jnp.exp(cst[length - 16 :]), slice(None))[15:16]
    for k in range(chunks):
        cut = slice(k * CHUNK, (k + 1) * CHUNK)
        mids[k] = jnp.broadcast_to(later[:, cut], (8, CHUNK))
        decays[k] = jnp.broadcast_to(ended[:, cut], (8, CHUNK))

    def to_partner(i):
        return pltpu.make_async_remote_copy(
            src_ref=part_send.at[i],
            dst_ref=part_recv.at[i],
            send_sem=psend.at[i],
            recv_sem=precv.at[i],
            device_id=(partner, t),
            device_id_type=MESH,
        )

    rows = lax.broadcasted_iota(jnp.int32, (EXTRA, PIECE), 0)

    def chain(i, r):
        return pltpu.make_async_remote_copy(
            src_ref=chain_send.at[i, pl.ds(r * ROWS, ROWS)],
            dst_ref=chain_recv.at[i, pl.ds(r * ROWS, ROWS)],
            send_sem=csend.at[i, r],
            recv_sem=crecv.at[i, r],
            device_id=(s + 2, t),
            device_id_type=MESH,
        )

    def share(i, where):
        return pltpu.make_async_remote_copy(
            src_ref=share_send.at[i],
            dst_ref=entering.at[where * half * pieces + i],
            send_sem=ssend.at[i],
            recv_sem=srecv.at[i],
            device_id=(partner, t),
            device_id_type=MESH,
        )

    odd = core == 1

    def each(begin, count, act):
        def one(i, carry):
            act(i)
            return carry

        lax.fori_loop(begin, begin + count, one, 0)


    def join(i):
        k = half * core + i // pieces
        cut = pl.ds(pl.multiple_of(lax.rem(i, pieces) * PIECE, PIECE), PIECE)
        to_partner(i).wait_recv()
        theirs = part_recv[i, 0:state, :].astype(jnp.float32)
        tail = part_recv[i, state : state + EXTRA, :].astype(jnp.float32)
        their_decay = tail[0:1] + tail[1:2]
        mine = states[k, :, cut]
        my_decay = decays[k, 0:1, cut]
        first = jnp.where(odd, theirs, mine)
        second = jnp.where(odd, mine, theirs)
        first_decay = jnp.where(odd, their_decay, my_decay)
        second_decay = jnp.where(odd, my_decay, their_decay)
        total = second_decay * first + second

        @pl.when((pair == 0) & (pairs > 1))
        def _():
            chain_send[i] = total.astype(jnp.bfloat16)
            for r in range(parts):
                chain(i, r).start()

        pair_state[i] = total
        pair_decay[i] = jnp.broadcast_to(second_decay * first_decay, (8, PIECE))
        middle[i] = first
        first_decays[i] = jnp.broadcast_to(first_decay, (8, PIECE))

    def step(i, entry):
        place = core * half * pieces + i
        if entry:
            for r in range(parts):
                band = slice(r * ROWS, (r + 1) * ROWS)
                chain(i, r).wait_recv()
                came = chain_recv[i, band, :].astype(jnp.float32)

                @pl.when(pair < pairs - 1)
                def _():
                    leaving = pair_decay[i][0:1] * came + pair_state[i, band, :]
                    chain_send[i, band, :] = leaving.astype(jnp.bfloat16)
                    chain(i, r).start()

                between = first_decays[i][0:1] * came + middle[i, band, :]
                share_send[i, band, :] = jnp.where(odd, came, between).astype(jnp.bfloat16)
                entering[place, band, :] = jnp.where(odd, between, came).astype(jnp.bfloat16)
        else:
            came = jnp.zeros((state, PIECE), jnp.float32)
            between = middle[i]
            share_send[i] = jnp.where(odd, came, between).astype(jnp.bfloat16)
            entering[place] = jnp.where(odd, between, came).astype(jnp.bfloat16)
        share(i, core).start()

    def first_join(j):
        @pl.when(pair == 0)
        def _():
            each(j * pieces, pieces, join)

    for j in range(half):
        for mine in range(2):
            k = half * (core if mine else 1 - core) + j
            project(HALO + q, HALO + length, pl.ds(pl.multiple_of(k * CHUNK, CHUNK), CHUNK))
            made = mids[k][0:1] * states[k] + half_state(k, 1, bt1, faded1)
            if mine:
                states[k] = made
                continue
            hi, lo = split(decays[k][0:1])
            hi, lo = hi.astype(jnp.float32), lo.astype(jnp.float32)
            for e in range(pieces):
                cut = slice(e * PIECE, (e + 1) * PIECE)
                tail = jnp.where(rows == 0, hi[:, cut], jnp.where(rows == 1, lo[:, cut], 0.0))
                part_send[j * pieces + e, 0:state, :] = made[:, cut].astype(jnp.bfloat16)
                part_send[j * pieces + e, state : state + EXTRA, :] = tail.astype(jnp.bfloat16)
                to_partner(j * pieces + e).start()
            if j > 0:
                first_join(j - 1)
    first_join(half - 1)

    cm = conv(inner + state, state, 0, length).astype(jnp.bfloat16)
    bt = jnp.concatenate([bt0, bt1], axis=1)
    dt = jnp.concatenate([dt0, dt1], axis=1)
    cs2 = cs * LOG2E
    cs2t = cst * LOG2E
    row2 = jnp.where(dt > 0.0, cs2 - jnp.log(dt) * LOG2E, 3e38)
    for k in range(chunks):
        steep[k] = cs2t[:, k * per : (k + 1) * per]
        rise[k] = row2[k * per : (k + 1) * per, :]
    scores = dot(cm, bt)
    top = jnp.where(keep, scores[:q, :q], 0.0)
    side = scores[q:, :q]
    end = jnp.where(keep, scores[q:, q:], 0.0)

    def mix_of(columns_k, rows_k, h):
        c0, c1 = columns_k[:q, h : h + 1], columns_k[q:, h : h + 1]
        r0, r1 = rows_k[h : h + 1, :q], rows_k[h : h + 1, q:]
        m0 = jnp.where(keep, top * jnp.exp2(c0 - r0), 0.0).astype(jnp.bfloat16)
        m1 = (side * jnp.exp2(c1 - r0)).astype(jnp.bfloat16)
        m2 = jnp.where(keep, end * jnp.exp2(c1 - r1), 0.0).astype(jnp.bfloat16)
        return m0, jnp.concatenate([m1, m2], axis=1)

    def intra(k):
        columns_k, rows_k = steep[k], rise[k]
        for p in range(per // 2):
            pairx = xs[k, :, p * 2 * head_dim : (p + 1) * 2 * head_dim]
            got = []
            for e in range(2):
                m0, m1 = mix_of(columns_k, rows_k, 2 * p + e)
                got.append(jnp.concatenate([dot(m0, pairx[:q]), dot(m1, pairx)], axis=0))
            y_in[k, :, p * 2 * head_dim : (p + 1) * 2 * head_dim] = jnp.where(low, got[0], got[1])

    def one_chunk(k, carry):
        intra(k)

        @pl.when((k == 0) & (pair > 0))
        def _():
            each(0, half * pieces, join)

        @pl.when((k == 0) & (pair == 0))
        def _():
            each(0, half * pieces, lambda i: step(i, False))

        @pl.when((k != 1) & (k < chunks - 1) & (pair == jnp.maximum(k, 1)))
        def _():
            each(0, half * pieces, lambda i: step(i, True))

        return carry

    lax.fori_loop(0, chunks, one_chunk, 0)

    grown = expand(jnp.exp(cst), slice(None))
    for k in range(chunks):
        ecs[k] = grown[:, k * CHUNK : (k + 1) * CHUNK]
    loads[8].wait()
    gated = silu(dot(nm[HALO:, :], w_gate[...]).astype(jnp.bfloat16).astype(jnp.float32))
    for k in range(chunks):
        gate[k] = gated[:, k * CHUNK : (k + 1) * CHUNK]
    loads[9].wait()
    loads[10].wait()
    out_row[...] = norm_out[...][None, :]

    def finish(k, square, total):
        entry = jnp.concatenate([entering[k * pieces + e] for e in range(pieces)], axis=1)
        start = pl.multiple_of(k * CHUNK, CHUNK)
        g = (y_in[k] + ecs[k] * dot(cm, entry)) * gate[k]
        square = square + jnp.sum(g * g, axis=-1, keepdims=True)
        scaled = (g * out_row[:, pl.ds(start, CHUNK)]).astype(jnp.bfloat16)
        return square, total + dot(scaled, w_out[pl.ds(start, CHUNK), :])

    square = jnp.zeros((length, 1), jnp.float32)
    total = jnp.zeros((length, out.shape[1]), jnp.float32)
    def last_chunk(n, carry):
        @pl.when((n < half) & (pair >= chunks - 1))
        def _():
            each(n * pieces, pieces, lambda i: step(i, True))

        @pl.when(n >= half)
        def _():
            for e in range(pieces):
                share((n - half) * pieces + e, 1 - core).wait_recv()

        return finish(lax.rem(half * core + n, chunks), *carry)

    square, total = lax.fori_loop(0, chunks, last_chunk, (square, total))
    out[...] = (total * lax.rsqrt(square / inner + epsilon)).astype(out.dtype)

    for peer in peers:
        for r in range(2):
            across(r, peer, t).wait_send()

    @pl.when(s < seqs - 1)
    def _():
        for h in range(tables):
            rim(s + 1, h, t).wait_send()

    for i in range(half * pieces):
        to_partner(i).wait_send()
        share(i, core).wait_send()

    @pl.when(pair < pairs - 1)
    def _():
        for i in range(half * pieces):
            for r in range(parts):
                chain(i, r).wait_send()


def local(tables, seqs, *args):
    args = args[:5] + (args[5].T,) + args[6:]
    columns, gaps, norm_in, w_gate, w_xbc, w_step = args[:6]
    step_bias, conv_weight, conv_bias, rates, norm_out, w_out = args[6:]
    length = columns.shape[1]
    inner = w_gate.shape[1]
    state = (w_xbc.shape[1] - inner) // 2
    chunks = inner // CHUNK
    per = rates.shape[0] // chunks
    count = chunks // 2 * (CHUNK // PIECE)
    f32, bf16 = jnp.float32, jnp.bfloat16
    dma = pltpu.SemaphoreType.DMA
    scratch = [pltpu.VMEM(a.shape, a.dtype) for a in args[1:]]
    scratch += [
        pltpu.VMEM((tables, HALO + length, columns.shape[2]), bf16),
        pltpu.VMEM((HALO + length, w_xbc.shape[1]), f32),
        pltpu.VMEM((chunks, length, CHUNK), bf16),
        pltpu.VMEM((chunks, length, CHUNK), f32),
        pltpu.VMEM((chunks, length, CHUNK), f32),
        pltpu.VMEM((chunks, length, CHUNK), f32),
        pltpu.VMEM((chunks, state, CHUNK), f32),
        pltpu.VMEM((chunks, 8, CHUNK), f32),
        pltpu.VMEM((count, state, PIECE), f32),
        pltpu.VMEM((count, 8, PIECE), f32),
        pltpu.VMEM((count, 8, PIECE), f32),
        pltpu.VMEM((count, state, PIECE), f32),
        pltpu.VMEM((2 * count, state, PIECE), bf16),
        pltpu.VMEM((count, state + EXTRA, PIECE), bf16),
        pltpu.VMEM((count, state + EXTRA, PIECE), bf16),
        pltpu.VMEM((count, state, PIECE), bf16),
        pltpu.VMEM((count, state, PIECE), bf16),
        pltpu.VMEM((count, state, PIECE), bf16),
        pltpu.VMEM((rates.shape[0], inner), bf16),
        pltpu.VMEM((HALO + length, w_gate.shape[0]), bf16),
        pltpu.VMEM((chunks, 8, CHUNK), f32),
        pltpu.VMEM((chunks, length, per), f32),
        pltpu.VMEM((chunks, per, length), f32),
        pltpu.VMEM((1, w_xbc.shape[1]), f32),
        pltpu.VMEM((1, inner), f32),
        dma((11,)),
        dma(()),
        dma((2, tables)),
        dma((2, tables)),
        dma((tables,)),
        dma((tables,)),
        dma((count,)),
        dma((count,)),
        dma((count, state // ROWS)),
        dma((count, state // ROWS)),
        dma((count,)),
        dma((count,)),
    ]
    got = pl.pallas_call(
        functools.partial(kernel, tables, seqs),
        out_shape=pltpu.VMEM((length, w_out.shape[1]), bf16),
        in_specs=[pl.BlockSpec(memory_space=pltpu.HBM)] * len(args),
        out_specs=pl.BlockSpec(memory_space=pltpu.VMEM),
        scratch_shapes=scratch,
        compiler_params=pltpu.CompilerParams(
            collective_id=0, has_side_effects=True, vmem_limit_bytes=60 * 10**6
        ),
        cost_estimate=pl.CostEstimate(
            flops=2 * 10**9, bytes_accessed=4 * 10**6, transcendentals=2 * 10**6
        ),
    )(*args)
    return got[None]


def solution(mesh):
    in_specs = (P(None, "seq", "table"), P("table", "seq")) + (P(),) * 10
    return jax.shard_map(
        functools.partial(local, mesh.shape["table"], mesh.shape["seq"]),
        mesh=mesh,
        in_specs=in_specs,
        out_specs=P("table", "seq", None),
        check_vma=False,
    )
```

```python
import functools

import jax
import jax.numpy as jnp
from jax import lax
from jax.experimental import pallas as pl
from jax.experimental.pallas import tpu as pltpu
from jax.sharding import PartitionSpec as P

MESH = pl.DeviceIdType.MESH
epsilon = 1e-05
LOG2E = 1.4426950408889634
HALO = 16
CHUNK = 256
PIECE = 128
ROWS = 64
EXTRA = 16


def silu(v):
    half = 0.5 * v
    return half + half * jnp.tanh(half)


def split(v):
    hi = v.astype(jnp.bfloat16)
    return hi, (v - hi.astype(jnp.float32)).astype(jnp.bfloat16)


def dot(a, b):
    return jnp.dot(a, b, preferred_element_type=jnp.float32)


def kernel(
    tables,
    seqs,
    columns,
    gaps_h,
    norm_in_h,
    w_gate_h,
    w_xbc_h,
    w_step_h,
    step_bias_h,
    conv_weight_h,
    conv_bias_h,
    rates_h,
    norm_out_h,
    w_out_h,
    out,
    gaps,
    norm_in,
    w_gate,
    w_xbc,
    w_step,
    step_bias,
    conv_weight,
    conv_bias,
    rates,
    norm_out,
    w_out,
    cols,
    xb,
    xs,
    y_in,
    ecs,
    gate,
    states,
    decays,
    pair_state,
    pair_decay,
    first_decays,
    middle,
    entering,
    part_send,
    part_recv,
    chain_send,
    chain_recv,
    share_send,
    spread_s,
    nm,
    mids,
    steep,
    rise,
    bias_row,
    out_row,
    load_sem,
    own_sem,
    all_send,
    all_recv,
    halo_send,
    halo_recv,
    psend,
    precv,
    csend,
    crecv,
    ssend,
    srecv,
):
    s = lax.axis_index("seq")
    t = lax.axis_index("table")
    core = lax.rem(s, 2)
    pair = s // 2
    pairs = seqs // 2
    partner = s + 1 - 2 * core
    length = gaps.shape[1]
    inner = w_gate.shape[1]
    heads = rates.shape[0]
    pieces = CHUNK // PIECE
    head_dim = inner // heads
    state = (w_xbc.shape[1] - inner) // 2
    parts = state // ROWS
    taps = conv_weight.shape[0]
    chunks = inner // CHUNK
    half = chunks // 2
    per = CHUNK // head_dim

    sources = (w_xbc_h, w_step_h, norm_in_h, conv_weight_h, conv_bias_h, gaps_h)
    sources += (rates_h, step_bias_h, w_gate_h, norm_out_h, w_out_h)
    places = (w_xbc, w_step, norm_in, conv_weight, conv_bias, gaps)
    places += (rates, step_bias, w_gate, norm_out, w_out)
    loads = [
        pltpu.make_async_copy(a, b, load_sem.at[i])
        for i, (a, b) in enumerate(zip(sources, places))
    ]
    own = pltpu.make_async_copy(columns.at[t], cols.at[t, pl.ds(HALO, length)], own_sem)

    barrier = pltpu.get_barrier_semaphore()

    def greet(where):
        pl.semaphore_signal(barrier, inc=1, device_id=where, device_id_type=MESH)

    for off in range(1, tables):
        greet((s, lax.rem(t + off, tables)))
    for h in range(tables):
        greet((partner, h))

    own.start()
    for load in loads:
        load.start()

    @pl.when(s == 0)
    def _():
        for h in range(tables):
            cols[h, 0:HALO, :] = jnp.zeros((HALO, cols.shape[2]), cols.dtype)

    def count(held):
        return jnp.where(held, 1, 0)

    earlier = count(pair > 0)
    pl.semaphore_wait(
        barrier, 2 * tables - 1 + earlier * (1 + tables * (1 - core))
    )

    q = length // 2

    def across(r, peer, sender):
        return pltpu.make_async_remote_copy(
            src_ref=columns.at[peer, pl.ds(r * q, q)],
            dst_ref=cols.at[sender, pl.ds(HALO + r * q, q)],
            send_sem=all_send.at[r, peer],
            recv_sem=all_recv.at[r, sender],
            device_id=(s, peer),
            device_id_type=MESH,
        )

    def rim(target, peer, sender):
        return pltpu.make_async_remote_copy(
            src_ref=columns.at[peer, pl.ds(length - HALO, HALO)],
            dst_ref=cols.at[sender, pl.ds(0, HALO)],
            send_sem=halo_send.at[peer],
            recv_sem=halo_recv.at[sender],
            device_id=(target, peer),
            device_id_type=MESH,
        )

    peers = [lax.rem(t + off, tables) for off in range(1, tables)]
    for peer in peers:
        across(0, peer, t).start()

    @pl.when(core == 0)
    def _():
        for h in range(tables):
            rim(s + 1, h, t).start()

    for peer in peers:
        across(1, peer, t).start()

    @pl.when(pair < pairs - 1)
    def _():
        greet((s + 2, t))

    @pl.when((pair < pairs - 1) & (core == 1))
    def _():
        for h in range(tables):
            greet((s + 1, h))

    @pl.when(pair > 0)
    def _():
        greet((s - 2, t))

    @pl.when((pair > 0) & (core == 0))
    def _():
        for h in range(tables):
            greet((s - 1, h))

    lane = lax.broadcasted_iota(jnp.int32, (heads, inner), 1) // head_dim
    head = lax.broadcasted_iota(jnp.int32, (heads, inner), 0)
    spread_s[...] = jnp.where(lane == head, 1.0, 0.0).astype(jnp.bfloat16)
    before = lax.broadcasted_iota(jnp.int32, (q, q), 0)
    after = lax.broadcasted_iota(jnp.int32, (q, q), 1)
    upper = jnp.where(before <= after, 1.0, 0.0).astype(jnp.bfloat16)
    keep = lax.broadcasted_iota(jnp.int32, (q, q), 0) >= lax.broadcasted_iota(
        jnp.int32, (q, q), 1
    )
    low = lax.broadcasted_iota(jnp.int32, (length, 2 * head_dim), 1) < head_dim

    def expand(v, lanes):
        hi, lo = split(v)
        return dot(hi, spread_s[:, lanes]) + dot(lo, spread_s[:, lanes])

    @pl.when(pair < pairs - 1)
    def _():
        pl.semaphore_wait(barrier, 1 + tables * core)

    @pl.when((pair < pairs - 1) & (core == 1))
    def _():
        for h in range(tables):
            rim(s + 1, h, t).start()

    for load in loads[:8]:
        load.wait()
    own.wait()
    bias_row[...] = conv_bias[...][None, :]

    def norm(begin, end):
        u = jnp.concatenate([cols[h, begin:end, :] for h in range(tables)], axis=1)
        u = u.astype(jnp.float32)
        scale = lax.rsqrt(jnp.mean(u * u, axis=-1, keepdims=True) + epsilon)
        nm[begin:end, :] = (u * scale * norm_in[...][None, :]).astype(jnp.bfloat16)

    def project(begin, end, lanes):
        made = dot(nm[begin:end, :], w_xbc[:, lanes])
        xb[begin:end, lanes] = made.astype(jnp.bfloat16).astype(jnp.float32)

    for peer in peers:
        across(0, peer, peer).wait_recv()

    @pl.when(s > 0)
    def _():
        for h in range(tables):
            rim(s, h, h).wait_recv()

    def times(g):
        here = nm[HALO + g * q : HALO + (g + 1) * q, :]
        raw = lax.dot_general(
            w_step[...], here, (((1,), (1,)), ((), ())), preferred_element_type=jnp.float32
        )
        raw = raw + step_bias[...][:, None]
        dt = jnp.maximum(raw, 0.0) + jnp.log1p(jnp.exp(-jnp.abs(raw)))
        da = -rates[...][:, None] * dt * gaps[:, g * q : (g + 1) * q]
        d1 = da.astype(jnp.bfloat16)
        d2, d3 = split(da - d1.astype(jnp.float32))
        cs = dot(d1, upper) + (dot(d2, upper) + dot(d3, upper))
        faded = (jnp.exp(cs[:, q - 1 : q] - cs) * dt).T
        return dt, cs, faded

    def conv(start, width, begin, count):
        lanes = pl.ds(start, width)
        total = bias_row[:, lanes]
        for k in range(taps):
            total = total + conv_weight[pl.ds(k, 1), lanes] * xb[
                pl.ds(HALO - taps + 1 + k + begin, count), lanes
            ]
        return silu(total)

    def half_state(k, g, bt, faded):
        start = k * CHUNK if g == 0 else pl.multiple_of(k * CHUNK, CHUNK)
        x = conv(start, CHUNK, g * q, q).astype(jnp.bfloat16)
        xs[k, g * q : (g + 1) * q, :] = x
        weighted = expand(faded, pl.ds(start, CHUNK)) * x.astype(jnp.float32)
        return dot(bt, weighted.astype(jnp.bfloat16))

    norm(0, HALO + q)
    project(0, HALO + q, slice(None))
    dt0, cs0, faded0 = times(0)
    bt0 = conv(inner, state, 0, q).T.astype(jnp.bfloat16)
    for k in range(chunks):
        states[k] = half_state(k, 0, bt0, faded0)

    for peer in peers:
        across(1, peer, peer).wait_recv()
    norm(HALO + q, HALO + length)
    dt1, cs1, faded1 = times(1)
    project(HALO + q, HALO + length, slice(inner, inner + 2 * state))
    bt1 = conv(inner, state, q, q).T.astype(jnp.bfloat16)
    closed = cs0[:, q - 1 : q]
    cs = jnp.concatenate([cs0, cs1 + closed], axis=1)
    cst = cs.T
    later = expand(jnp.exp(cs1.T[q - 16 :]), slice(None))[15:16]
    ended = expand(jnp.exp(cst[length - 16 :]), slice(None))[15:16]
    for k in range(chunks):
        cut = slice(k * CHUNK, (k + 1) * CHUNK)
        mids[k] = jnp.broadcast_to(later[:, cut], (8, CHUNK))
        decays[k] = jnp.broadcast_to(ended[:, cut], (8, CHUNK))

    def to_partner(i):
        return pltpu.make_async_remote_copy(
            src_ref=part_send.at[i],
            dst_ref=part_recv.at[i],
            send_sem=psend.at[i],
            recv_sem=precv.at[i],
            device_id=(partner, t),
            device_id_type=MESH,
        )

    rows = lax.broadcasted_iota(jnp.int32, (EXTRA, PIECE), 0)

    def chain(i, r):
        return pltpu.make_async_remote_copy(
            src_ref=chain_send.at[i, pl.ds(r * ROWS, ROWS)],
            dst_ref=chain_recv.at[i, pl.ds(r * ROWS, ROWS)],
            send_sem=csend.at[i, r],
            recv_sem=crecv.at[i, r],
            device_id=(s + 2, t),
            device_id_type=MESH,
        )

    def share(i, where):
        return pltpu.make_async_remote_copy(
            src_ref=share_send.at[i],
            dst_ref=entering.at[where * half * pieces + i],
            send_sem=ssend.at[i],
            recv_sem=srecv.at[i],
            device_id=(partner, t),
            device_id_type=MESH,
        )

    odd = core == 1

    def each(begin, count, act):
        def one(i, carry):
            act(i)
            return carry

        lax.fori_loop(begin, begin + count, one, 0)


    def join(i):
        k = half * core + i // pieces
        cut = pl.ds(pl.multiple_of(lax.rem(i, pieces) * PIECE, PIECE), PIECE)
        to_partner(i).wait_recv()
        theirs = part_recv[i, 0:state, :].astype(jnp.float32)
        tail = part_recv[i, state : state + EXTRA, :].astype(jnp.float32)
        their_decay = tail[0:1] + tail[1:2]
        mine = states[k, :, cut]
        my_decay = decays[k, 0:1, cut]
        first = jnp.where(odd, theirs, mine)
        second = jnp.where(odd, mine, theirs)
        first_decay = jnp.where(odd, their_decay, my_decay)
        second_decay = jnp.where(odd, my_decay, their_decay)
        total = second_decay * first + second

        @pl.when((pair == 0) & (pairs > 1))
        def _():
            chain_send[i] = total.astype(jnp.bfloat16)
            for r in range(parts):
                chain(i, r).start()

        pair_state[i] = total
        pair_decay[i] = jnp.broadcast_to(second_decay * first_decay, (8, PIECE))
        middle[i] = first
        first_decays[i] = jnp.broadcast_to(first_decay, (8, PIECE))

    def forward(i):
        for r in range(parts):
            band = slice(r * ROWS, (r + 1) * ROWS)
            chain(i, r).wait_recv()

            @pl.when(pair < pairs - 1)
            def _():
                came = chain_recv[i, band, :].astype(jnp.float32)
                leaving = pair_decay[i][0:1] * came + pair_state[i, band, :]
                chain_send[i, band, :] = leaving.astype(jnp.bfloat16)
                chain(i, r).start()

    def step(i, entry):
        place = core * half * pieces + i
        if entry:
            came = chain_recv[i].astype(jnp.float32)
            between = first_decays[i][0:1] * came + middle[i]
        else:
            came = jnp.zeros((state, PIECE), jnp.float32)
            between = middle[i]
        share_send[i] = jnp.where(odd, came, between).astype(jnp.bfloat16)
        entering[place] = jnp.where(odd, between, came).astype(jnp.bfloat16)
        share(i, core).start()

    def first_join(j):
        @pl.when(pair == 0)
        def _():
            each(j * pieces, pieces, join)

    for j in range(half):
        for mine in range(2):
            k = half * (core if mine else 1 - core) + j
            project(HALO + q, HALO + length, pl.ds(pl.multiple_of(k * CHUNK, CHUNK), CHUNK))
            made = mids[k][0:1] * states[k] + half_state(k, 1, bt1, faded1)
            if mine:
                states[k] = made
                continue
            hi, lo = split(decays[k][0:1])
            hi, lo = hi.astype(jnp.float32), lo.astype(jnp.float32)
            for e in range(pieces):
                cut = slice(e * PIECE, (e + 1) * PIECE)
                tail = jnp.where(rows == 0, hi[:, cut], jnp.where(rows == 1, lo[:, cut], 0.0))
                part_send[j * pieces + e, 0:state, :] = made[:, cut].astype(jnp.bfloat16)
                part_send[j * pieces + e, state : state + EXTRA, :] = tail.astype(jnp.bfloat16)
                to_partner(j * pieces + e).start()
            if j > 0:
                first_join(j - 1)
    first_join(half - 1)

    cm = conv(inner + state, state, 0, length).astype(jnp.bfloat16)
    bt = jnp.concatenate([bt0, bt1], axis=1)
    dt = jnp.concatenate([dt0, dt1], axis=1)
    cs2 = cs * LOG2E
    cs2t = cst * LOG2E
    row2 = jnp.where(dt > 0.0, cs2 - jnp.log(dt) * LOG2E, 3e38)
    for k in range(chunks):
        steep[k] = cs2t[:, k * per : (k + 1) * per]
        rise[k] = row2[k * per : (k + 1) * per, :]
    scores = dot(cm, bt)
    top = jnp.where(keep, scores[:q, :q], 0.0)
    side = scores[q:, :q]
    end = jnp.where(keep, scores[q:, q:], 0.0)

    def mix_of(columns_k, rows_k, h):
        c0, c1 = columns_k[:q, h : h + 1], columns_k[q:, h : h + 1]
        r0, r1 = rows_k[h : h + 1, :q], rows_k[h : h + 1, q:]
        m0 = jnp.where(keep, top * jnp.exp2(c0 - r0), 0.0).astype(jnp.bfloat16)
        m1 = (side * jnp.exp2(c1 - r0)).astype(jnp.bfloat16)
        m2 = jnp.where(keep, end * jnp.exp2(c1 - r1), 0.0).astype(jnp.bfloat16)
        return m0, jnp.concatenate([m1, m2], axis=1)

    def intra(k):
        columns_k, rows_k = steep[k], rise[k]
        for p in range(per // 2):
            pairx = xs[k, :, p * 2 * head_dim : (p + 1) * 2 * head_dim]
            got = []
            for e in range(2):
                m0, m1 = mix_of(columns_k, rows_k, 2 * p + e)
                got.append(jnp.concatenate([dot(m0, pairx[:q]), dot(m1, pairx)], axis=0))
            y_in[k, :, p * 2 * head_dim : (p + 1) * 2 * head_dim] = jnp.where(low, got[0], got[1])

    def one_chunk(k, carry):
        intra(k)

        @pl.when((k == 0) & (pair > 0))
        def _():
            each(0, half * pieces, join)

        @pl.when((k == 0) & (pair == 0))
        def _():
            each(0, half * pieces, lambda i: step(i, False))

        @pl.when((k != 1) & (k < chunks - 1) & (pair == jnp.maximum(k, 1)))
        def _():
            each(0, half * pieces, forward)
            each(0, half * pieces, lambda i: step(i, True))

        return carry

    lax.fori_loop(0, chunks, one_chunk, 0)

    grown = expand(jnp.exp(cst), slice(None))
    for k in range(chunks):
        ecs[k] = grown[:, k * CHUNK : (k + 1) * CHUNK]
    loads[8].wait()
    gated = silu(dot(nm[HALO:, :], w_gate[...]).astype(jnp.bfloat16).astype(jnp.float32))
    for k in range(chunks):
        gate[k] = gated[:, k * CHUNK : (k + 1) * CHUNK]
    loads[9].wait()
    loads[10].wait()
    out_row[...] = norm_out[...][None, :]

    def finish(k, square, total):
        entry = jnp.concatenate([entering[k * pieces + e] for e in range(pieces)], axis=1)
        start = pl.multiple_of(k * CHUNK, CHUNK)
        g = (y_in[k] + ecs[k] * dot(cm, entry)) * gate[k]
        square = square + jnp.sum(g * g, axis=-1, keepdims=True)
        scaled = (g * out_row[:, pl.ds(start, CHUNK)]).astype(jnp.bfloat16)
        return square, total + dot(scaled, w_out[pl.ds(start, CHUNK), :])

    square = jnp.zeros((length, 1), jnp.float32)
    total = jnp.zeros((length, out.shape[1]), jnp.float32)
    for n in range(chunks):
        if n < half:

            @pl.when(pair >= chunks - 1)
            def _():
                each(n * pieces, pieces, lambda i: (forward(i), step(i, True)))

        else:
            for e in range(pieces):
                share((n - half) * pieces + e, 1 - core).wait_recv()
        square, total = finish(lax.rem(half * core + n, chunks), square, total)
    out[...] = (total * lax.rsqrt(square / inner + epsilon)).astype(out.dtype)

    for peer in peers:
        for r in range(2):
            across(r, peer, t).wait_send()

    @pl.when(s < seqs - 1)
    def _():
        for h in range(tables):
            rim(s + 1, h, t).wait_send()

    for i in range(half * pieces):
        to_partner(i).wait_send()
        share(i, core).wait_send()

    @pl.when(pair < pairs - 1)
    def _():
        for i in range(half * pieces):
            for r in range(parts):
                chain(i, r).wait_send()


def local(tables, seqs, *args):
    args = args[:5] + (args[5].T,) + args[6:]
    columns, gaps, norm_in, w_gate, w_xbc, w_step = args[:6]
    step_bias, conv_weight, conv_bias, rates, norm_out, w_out = args[6:]
    length = columns.shape[1]
    inner = w_gate.shape[1]
    state = (w_xbc.shape[1] - inner) // 2
    chunks = inner // CHUNK
    per = rates.shape[0] // chunks
    count = chunks // 2 * (CHUNK // PIECE)
    f32, bf16 = jnp.float32, jnp.bfloat16
    dma = pltpu.SemaphoreType.DMA
    scratch = [pltpu.VMEM(a.shape, a.dtype) for a in args[1:]]
    scratch += [
        pltpu.VMEM((tables, HALO + length, columns.shape[2]), bf16),
        pltpu.VMEM((HALO + length, w_xbc.shape[1]), f32),
        pltpu.VMEM((chunks, length, CHUNK), bf16),
        pltpu.VMEM((chunks, length, CHUNK), f32),
        pltpu.VMEM((chunks, length, CHUNK), f32),
        pltpu.VMEM((chunks, length, CHUNK), f32),
        pltpu.VMEM((chunks, state, CHUNK), f32),
        pltpu.VMEM((chunks, 8, CHUNK), f32),
        pltpu.VMEM((count, state, PIECE), f32),
        pltpu.VMEM((count, 8, PIECE), f32),
        pltpu.VMEM((count, 8, PIECE), f32),
        pltpu.VMEM((count, state, PIECE), f32),
        pltpu.VMEM((2 * count, state, PIECE), bf16),
        pltpu.VMEM((count, state + EXTRA, PIECE), bf16),
        pltpu.VMEM((count, state + EXTRA, PIECE), bf16),
        pltpu.VMEM((count, state, PIECE), bf16),
        pltpu.VMEM((count, state, PIECE), bf16),
        pltpu.VMEM((count, state, PIECE), bf16),
        pltpu.VMEM((rates.shape[0], inner), bf16),
        pltpu.VMEM((HALO + length, w_gate.shape[0]), bf16),
        pltpu.VMEM((chunks, 8, CHUNK), f32),
        pltpu.VMEM((chunks, length, per), f32),
        pltpu.VMEM((chunks, per, length), f32),
        pltpu.VMEM((1, w_xbc.shape[1]), f32),
        pltpu.VMEM((1, inner), f32),
        dma((11,)),
        dma(()),
        dma((2, tables)),
        dma((2, tables)),
        dma((tables,)),
        dma((tables,)),
        dma((count,)),
        dma((count,)),
        dma((count, state // ROWS)),
        dma((count, state // ROWS)),
        dma((count,)),
        dma((count,)),
    ]
    got = pl.pallas_call(
        functools.partial(kernel, tables, seqs),
        out_shape=pltpu.VMEM((length, w_out.shape[1]), bf16),
        in_specs=[pl.BlockSpec(memory_space=pltpu.HBM)] * len(args),
        out_specs=pl.BlockSpec(memory_space=pltpu.VMEM),
        scratch_shapes=scratch,
        compiler_params=pltpu.CompilerParams(
            collective_id=0, has_side_effects=True, vmem_limit_bytes=60 * 10**6
        ),
        cost_estimate=pl.CostEstimate(
            flops=2 * 10**9, bytes_accessed=4 * 10**6, transcendentals=2 * 10**6
        ),
    )(*args)
    return got[None]


def solution(mesh):
    in_specs = (P(None, "seq", "table"), P("table", "seq")) + (P(),) * 10
    return jax.shard_map(
        functools.partial(local, mesh.shape["table"], mesh.shape["seq"]),
        mesh=mesh,
        in_specs=in_specs,
        out_specs=P("table", "seq", None),
        check_vma=False,
    )
```
